256 devices in a mesh: dp: 8 (over z), vocab: 32 (over x, y, core).
Axes of the slice: x: 4, y: 4, z: 8, core: 2. Of those that a mesh axis runs over, the one named last changes fastest.
Arguments:
- hidden: bfloat16 [1024, 8192], P('vocab', 'dp'), as said below
- labels: int32 [1024], P('dp'), may hold values from 0 to 65535
- head_weight: bfloat16 [65536, 8192], P('vocab', 'dp'), as said below
- hess_old: bfloat16 [65536, 8192], P('vocab', 'dp'), may hold values from 2.712477e-08 to 2.7008355e-07
Outputs:
- update: bfloat16 [65536, 8192], P('vocab', 'dp')
The draws below stay inside these ranges and needn't reach their ends.
Inputs may be any that keep to these rules, and one draw needn't show every extreme that they name: hidden holds entries of order one, at most 8 in magnitude. head_weight holds entries of magnitude about 3 / sqrt(8192).
All inputs are finite; a program needn't handle non-finite values.
Results may differ from the reference program's by a relative error of at most 0.006.
Values may be sent and summed in bfloat16 or wider, within the bound.
A program may use at most 64 MiB of HBM per device.

```python
import math
import jax
import jax.numpy as jnp
from jax import lax

D = 8192
V_DEV = 2048
TOKENS = 1024
VOCAB = 65536


def weight_rows(key):
    return 3.0 * jax.random.normal(key, (VOCAB, D), jnp.float32) / math.sqrt(D)


def draw_head_weight(key, part):
    rows = weight_rows(key)
    return rows.astype(jnp.bfloat16)


def draw_hidden(key, part):
    key = jax.random.fold_in(key, 7)
    keys = jax.random.split(key, 1)
    values = 0.5 * jax.random.normal(keys[0], (TOKENS, D), jnp.float32)
    return jnp.clip(values, -8.0, 8.0).astype(jnp.bfloat16)


def touch_ends(values, stream_key, low, top_value):
    spot = [jax.random.randint(jax.random.fold_in(stream_key, axis), (), 0, length) for axis, length in enumerate(values.shape)]
    main_axis = values.shape.index(max(values.shape))
    neighbour = spot[:main_axis] + [(spot[main_axis] + 1) % values.shape[main_axis]] + spot[main_axis + 1:]
    return values.at[tuple(spot)].set(low).at[tuple(neighbour)].set(top_value)


def levels(own_key, shape, pieces, least, high):
    loudness, own = 1.0, jax.random.fold_in(own_key, 6)
    for dim, blocks in pieces:
        steps = jnp.exp(jax.random.uniform(jax.random.fold_in(own, dim), (blocks,), jnp.float32, least / len(pieces), high / len(pieces)))
        loudness = loudness * jnp.repeat(steps, shape[dim] // blocks).reshape([-1 if axis == dim else 1 for axis in range(len(shape))])
    return loudness


def setup_inputs(seed: int = 0) -> dict:
    arg_keys = jax.random.split(jax.random.key(seed), 5)
    return {
        "hidden": draw_hidden(jax.random.fold_in(arg_keys[4], 71), 0),
        "labels": touch_ends(jax.random.randint(arg_keys[1], (TOKENS,), 0, VOCAB), jax.random.fold_in(arg_keys[1], 1), 0, VOCAB - 1).astype(jnp.int32),
        "head_weight": draw_head_weight(jax.random.fold_in(arg_keys[4], 71), 0),
        "hess_old": jnp.clip(jnp.exp(math.log(2.7008354663848877e-07) - 2.298284 * jax.random.uniform(arg_keys[3], (VOCAB, D), jnp.float32) ** levels(arg_keys[3], (VOCAB, D), ((0, 32), (1, 8)), -0.2, 0.2)), 2.7124769985675812e-08, 2.7008354663848877e-07).astype(jnp.bfloat16),
    }


def reference(hidden, labels, head_weight, hess_old):
    logits = jnp.dot(hidden, head_weight.T, preferred_element_type=jnp.float32)
    top = jnp.max(logits, axis=1, keepdims=True)
    expos = jnp.exp(logits - top)
    total = jnp.sum(expos, axis=1, keepdims=True)
    probs = expos / total
    columns = jnp.arange(VOCAB, dtype=jnp.int32)[None, :]
    onehot = (columns == labels[:, None]).astype(jnp.float32)
    resid = (probs - onehot).astype(jnp.bfloat16)
    blocks = VOCAB // V_DEV
    resid_blocks = resid.reshape(TOKENS, blocks, V_DEV).transpose(1, 0, 2)
    old_blocks = hess_old.reshape(blocks, V_DEV, D)

    def one_block(pair):
        resid_block, old_block = pair
        sums = jnp.dot(resid_block.T, hidden, preferred_element_type=jnp.float32)
        fresh = 0.9 * old_block.astype(jnp.float32) + 0.1 * sums * sums
        return jnp.clip(sums / (10000.0 * fresh), -1.0, 1.0).astype(jnp.bfloat16)

    updates = lax.map(one_block, (resid_blocks, old_blocks))
    return updates.reshape(VOCAB, D)
```

```python
import functools

import jax
import jax.numpy as jnp
from jax import lax
from jax.experimental import pallas as pl
from jax.experimental.pallas import tpu as pltpu
from jax.sharding import PartitionSpec as P

MESH = pl.DeviceIdType.MESH
F32, BF16, I16 = jnp.float32, jnp.bfloat16, jnp.int16
NZ, NX, NY = 8, 4, 4
OWN = 256
HALF = 128
SB = 256
TOK = 1024
WIDTH = 1024
BLK = 32
TOP = 32760.0
TINY = 1e-30


def kernel(
    hid_ref, lab_ref, w_ref, hess_ref, out_ref,
    w_v, hess_v, h_v, lab_v, part, mb, rb, rf, bb, lg, st, st_sib, st_pl, st_z, stat, res, ob,
    loc_sem, g_send, g_recv, f_send, f_recv, lab_send, lab_recv, rs_send, rs_recv, bs_send, bs_recv,
    ag_send, ag_recv, st_send, st_recv, sib_send, sib_recv, sz_send, sz_recv, out_sem,
):
    z = lax.axis_index("dp")
    v = lax.axis_index("vocab")
    core = lax.rem(v, 2)
    chip = v // 2
    x, y = chip // NY, lax.rem(chip, NY)
    sib = (z, v + 1 - 2 * core)

    def zmod(a):
        return lax.rem(a + 2 * NZ, NZ)

    def peer(xx, yy):
        return (z, (xx * NY + yy) * 2 + core)

    def remote(src, dst, ssem, rsem, dev):
        return pltpu.make_async_remote_copy(
            src_ref=src, dst_ref=dst, send_sem=ssem, recv_sem=rsem, device_id=dev, device_id_type=MESH
        )

    w_copy = pltpu.make_async_copy(w_ref, w_v, loc_sem.at[0])
    hess_copy = pltpu.make_async_copy(hess_ref, hess_v, loc_sem.at[1])
    lab_copy = pltpu.make_async_copy(lab_ref, lab_v.at[z], loc_sem.at[2])
    w_copy.start()
    lab_copy.start()

    zring = ((zmod(z + 1), v), (zmod(z - 1), v))
    zpeers = [(zmod(z + k), v) for k in range(1, NZ)]
    plane = [peer(x, lax.rem(y + d, NY)) for d in (1, 3, 2)]
    for dx in (3, 1, 2):
        plane += [peer(lax.rem(x + dx, NX), lax.rem(y + d, NY)) for d in range(NY)]

    barrier = pltpu.get_barrier_semaphore()
    for dev in zpeers + plane + [sib]:
        pl.semaphore_signal(barrier, inc=1, device_id=dev, device_id_type=MESH)
    pl.semaphore_wait(barrier, len(zpeers) + len(plane) + 1)

    def rows(c, co):
        return h_v.at[pl.ds(pl.multiple_of((c * 2 + co) * BLK, BLK), BLK)]

    own_copy = pltpu.make_async_copy(hid_ref, rows(chip, core), g_recv.at[chip])
    own_copy.start()
    gathers = [
        remote(hid_ref, rows(chip, core), g_send.at[k], g_recv.at[chip], dev) for k, dev in enumerate(plane)
    ]
    for g in gathers:
        g.start()
    labs = [
        remote(lab_ref, lab_v.at[z], lab_send.at[k], lab_recv.at[k], dev) for k, dev in enumerate(zpeers)
    ]
    for g in labs:
        g.start()
    hess_copy.start()
    w_copy.wait()

    def xs_of(i):
        off = i + jnp.where(i == 2, 1, 0) - jnp.where(i == 3, 1, 0)
        return lax.rem(x + off, NX)

    def forward(c):
        return remote(rows(c, core), rows(c, core), f_send.at[c], f_recv.at[c], sib)

    def gather_block(xs):
        def arrive(d, _):
            c = xs * NY + lax.rem(y + d, NY)
            pltpu.make_async_copy(hid_ref, rows(c, core), g_recv.at[c]).wait()
            forward(c).start()
            return 0

        lax.fori_loop(0, NY, arrive, 0)

        def other(d, _):
            c = xs * NY + lax.rem(y + d, NY)
            remote(rows(c, 1 - core), rows(c, 1 - core), f_send.at[c], f_recv.at[c], sib).wait_recv()
            return 0

        lax.fori_loop(0, NY, other, 0)

    def mm(xs, o):
        a = w_v[pl.ds(pl.multiple_of(o * OWN, OWN), OWN), :]
        b = h_v[pl.ds(pl.multiple_of(xs * SB, SB), SB), :]
        p = lax.dot_general(a, b, (((1,), (1,)), ((), ())), preferred_element_type=F32)
        part[xs, o] = p
        mb[xs, o, 0:1, :] = jnp.max(jnp.abs(p[:HALF]), axis=0, keepdims=True)
        mb[xs, o, 1:2, :] = jnp.max(jnp.abs(p[HALF:]), axis=0, keepdims=True)

    def rows_of(xs, o, half):
        return part[xs, o, half * HALF : (half + 1) * HALF, :]

    def to_int(q):
        return jnp.round(q).astype(I16)

    def first(d, xs, place, o, half):
        b = mb[xs, o, half : half + 1, :]
        scale = TOP / jnp.maximum(b, TINY)
        rb[d, xs, 0, place * HALF : (place + 1) * HALF, :] = to_int(rows_of(xs, o, half) * scale)
        bb[d, xs, 0, place : place + 1, :] = b

    def fold(d, xs, slot, place, o, half):
        b_in = bb[d, xs, slot, place : place + 1, :]
        b = b_in + mb[xs, o, half : half + 1, :]
        inv = 1.0 / jnp.maximum(b, TINY)
        got = rb[d, xs, slot, place * HALF : (place + 1) * HALF, :].astype(F32)
        q = got * (b_in * inv) + rows_of(xs, o, half) * (TOP * inv)
        rb[d, xs, slot, place * HALF : (place + 1) * HALF, :] = to_int(q)
        bb[d, xs, slot, place : place + 1, :] = b

    def rs_data(d, xs, s):
        if s < 4:
            src, dst = rb.at[d, xs, s - 1], rb.at[d, xs, s]
        else:
            src, dst = rb.at[d, xs, 3, pl.ds(0, HALF)], rf.at[d, xs]
        return remote(src, dst, rs_send.at[d, xs, s - 1], rs_recv.at[d, xs, s - 1], zring[d])

    def rs_bound(d, xs, s):
        return remote(
            bb.at[d, xs, s - 1], bb.at[d, xs, s], bs_send.at[d, xs, s - 1], bs_recv.at[d, xs, s - 1], zring[d]
        )

    def rs_start(d, xs, s):
        rs_bound(d, xs, s).start()
        rs_data(d, xs, s).start()

    def rs_wait(d, xs, s):
        rs_bound(d, xs, s).wait_recv()
        rs_data(d, xs, s).wait_recv()

    def step1(i, _):
        xs = xs_of(i)
        gather_block(xs)

        def owners(j, _):
            mm(xs, zmod(z + 3 + j))
            return 0

        lax.fori_loop(0, 3, owners, 0)
        first(0, xs, 0, zmod(z + 4), 0)
        first(0, xs, 1, zmod(z + 3), 1)
        rs_start(0, xs, 1)
        first(1, xs, 0, zmod(z - 4), 1)
        first(1, xs, 1, zmod(z - 3), 0)
        rs_start(1, xs, 1)
        return 0

    lax.fori_loop(0, NX, step1, 0)

    for s in (1, 2):

        def step(i, _, s=s):
            xs = xs_of(i)

            def owners(j, _):
                mm(xs, zmod(z + (3 - s) * (1 - 2 * j)))
                return 0

            lax.fori_loop(0, 2, owners, 0)
            rs_wait(0, xs, s)
            fold(0, xs, s, 0, zmod(z + 4 - s), 0)
            fold(0, xs, s, 1, zmod(z + 3 - s), 1)
            rs_start(0, xs, s + 1)
            rs_wait(1, xs, s)
            fold(1, xs, s, 0, zmod(z - 4 + s), 1)
            fold(1, xs, s, 1, zmod(z - 3 + s), 0)
            rs_start(1, xs, s + 1)
            return 0

        lax.fori_loop(0, NX, step, 0)

    def step4(i, _):
        xs = xs_of(i)
        rs_wait(0, xs, 3)
        fold(0, xs, 3, 0, zmod(z + 1), 0)
        rs_start(0, xs, 4)
        rs_wait(1, xs, 3)
        fold(1, xs, 3, 0, zmod(z - 1), 1)
        rs_start(1, xs, 4)
        mm(xs, z)
        return 0

    lax.fori_loop(0, NX, step4, 0)

    def ag(d, xs, s):
        o = zmod(z + 1 - s) if d == 0 else zmod(z - 1 + s)
        ref = lg.at[o, xs]
        if s == 4:
            ref = lg.at[o, xs, pl.ds(d * HALF, HALF)]
        return remote(ref, ref, ag_send.at[d, xs, s - 1], ag_recv.at[d, xs, s - 1], zring[d])

    def ag_wait(d, xs, s):
        o = zmod(z - s) if d == 0 else zmod(z + s)
        ref = lg.at[o, xs]
        if s == 4:
            ref = lg.at[o, xs, pl.ds(d * HALF, HALF)]
        remote(ref, ref, ag_send.at[d, xs, s - 1], ag_recv.at[d, xs, s - 1], zring[d]).wait_recv()

    def total(i, _):
        xs = xs_of(i)
        rs_wait(0, xs, 4)
        rs_wait(1, xs, 4)
        b0, b1 = bb[0, xs, 4, 0:1, :], bb[1, xs, 3, 1:2, :]
        c0, c1 = bb[1, xs, 4, 0:1, :], bb[0, xs, 3, 1:2, :]
        k = 1.0 / TOP
        upper = rows_of(xs, z, 0) + rf[0, xs].astype(F32) * (b0 * k) + rb[1, xs, 3, HALF:, :].astype(F32) * (b1 * k)
        lower = rows_of(xs, z, 1) + rf[1, xs].astype(F32) * (c0 * k) + rb[0, xs, 3, HALF:, :].astype(F32) * (c1 * k)
        b = jnp.maximum(mb[xs, z, 0:1, :] + b0 + b1, mb[xs, z, 1:2, :] + c0 + c1)
        b = jnp.maximum(b, TINY)
        scale = TOP / b
        lg[z, xs, :HALF, :] = to_int(upper * scale)
        lg[z, xs, HALF:, :] = to_int(lower * scale)
        ag(0, xs, 1).start()
        ag(1, xs, 1).start()
        m = jnp.maximum(jnp.max(upper, axis=0, keepdims=True), jnp.max(lower, axis=0, keepdims=True))
        e = jnp.sum(jnp.exp(upper - m), axis=0, keepdims=True) + jnp.sum(jnp.exp(lower - m), axis=0, keepdims=True)
        for j in range(2):
            lanes = slice(128 * j, 128 * (j + 1))
            st[pl.ds(2 * xs + j, 1), :] = m[:, lanes]
            st[pl.ds(8 + 2 * xs + j, 1), :] = e[:, lanes]
            st_z[z, pl.ds(16 + 2 * xs + j, 1), :] = b[:, lanes] * k
        return 0

    lax.fori_loop(0, NX, total, 0)

    def merge(a, b):
        m = jnp.maximum(a[0], b[0])
        return m, a[1] * jnp.exp(a[0] - m) + b[1] * jnp.exp(b[0] - m)

    sib_copy = remote(st, st_sib, sib_send, sib_recv, sib)
    sib_copy.start()
    sib_copy.wait()
    m, e = merge((st[0:8], st[8:16]), (st_sib[0:8], st_sib[8:16]))
    st_pl[chip, 0:8] = m
    st_pl[chip, 8:16] = e
    spreads = [
        remote(st_pl.at[chip], st_pl.at[chip], st_send.at[k], st_recv.at[chip], dev) for k, dev in enumerate(plane)
    ]
    for g in spreads:
        g.start()

    def ag_step(s):
        def body(i, _):
            xs = xs_of(i)
            for d in (0, 1):
                ag_wait(d, xs, s)
                ag(d, xs, s + 1).start()
            return 0

        lax.fori_loop(0, NX, body, 0)

    ag_step(1)

    def plane_wait(k, _):
        c = lax.rem(chip + k, NX * NY)
        remote(st_pl.at[c], st_pl.at[c], st_send.at[0], st_recv.at[c], sib).wait_recv()
        return 0

    lax.fori_loop(1, NX * NY, plane_wait, 0)
    m = st_pl[0, 0:8]
    for c in range(1, NX * NY):
        m = jnp.maximum(m, st_pl[c, 0:8])
    e = jnp.zeros_like(m)
    for c in range(NX * NY):
        e = e + st_pl[c, 8:16] * jnp.exp(st_pl[c, 0:8] - m)
    st_z[z, 0:8] = m
    st_z[z, 8:16] = e
    deep = [remote(st_z.at[z], st_z.at[z], sz_send.at[k], sz_recv.at[k], dev) for k, dev in enumerate(zpeers)]
    for g in deep:
        g.start()

    ag_step(2)

    for k in range(NZ - 1):
        o = zmod(z - 1 - k)
        remote(st_z.at[o], st_z.at[o], sz_send.at[k], sz_recv.at[k], sib).wait_recv()
        remote(lab_v.at[o], lab_v.at[o], lab_send.at[k], lab_recv.at[k], sib).wait_recv()
    lab_copy.wait()
    m = st_z[0, 0:8]
    for o in range(1, NZ):
        m = jnp.maximum(m, st_z[o, 0:8])
    e = jnp.zeros_like(m)
    for o in range(NZ):
        e = e + st_z[o, 8:16] * jnp.exp(st_z[o, 0:8] - m)
    stat[0:8] = m
    stat[8:16] = 1.0 / e
    hess_copy.wait()

    def unit(o):
        base = v * (NZ * OWN) + o * OWN
        for r in range(8):
            top, inv = stat[r : r + 1, :], stat[8 + r : 9 + r, :]
            scale = st_z[o, 16 + r : 17 + r, :]
            lab = lab_v[r]
            lanes = slice(128 * (r % 2), 128 * (r % 2 + 1))
            for q in range(4):
                sub = slice(64 * q, 64 * (q + 1))
                l = lg[o, r // 2, sub, lanes].astype(F32) * scale
                p = jnp.exp(l - top) * inv
                ids = base + 64 * q + lax.broadcasted_iota(jnp.int32, (64, 128), 0)
                res[sub, 128 * r : 128 * (r + 1)] = (p - (ids == lab).astype(F32)).astype(BF16)

        def tile(n, _):
            cols = pl.ds(pl.multiple_of(n * 256, 256), 256)
            sums = jnp.dot(res[...], h_v[:, cols], preferred_element_type=F32)
            rws = pl.ds(pl.multiple_of(o * OWN, OWN), OWN)
            fresh = 0.9 * hess_v[rws, cols].astype(F32) + 0.1 * sums * sums
            ob[rws, cols] = jnp.clip(sums / (10000.0 * fresh), -1.0, 1.0).astype(BF16)
            return 0

        lax.fori_loop(0, WIDTH // 256, tile, 0)
        out_copy(o).start()

    def out_copy(o):
        rws = pl.ds(pl.multiple_of(o * OWN, OWN), OWN)
        return pltpu.make_async_copy(ob.at[rws], out_ref.at[rws], out_sem.at[o])

    def last(k, _):
        xs = xs_of(lax.rem(k, NX))

        @pl.when(k < NX)
        def _():
            for d in (0, 1):
                ag_wait(d, xs, 3)
                ag(d, xs, 4).start()

        @pl.when(k == 7)
        def _():
            def tail(i, _):
                for d in (0, 1):
                    ag_wait(d, xs_of(i), 4)
                return 0

            lax.fori_loop(0, NX, tail, 0)

        near = (k + 1) // 2
        unit(zmod(z + near * (1 - 2 * lax.rem(k, 2))))
        return 0

    lax.fori_loop(0, NZ, last, 0)

    for g in gathers + labs + spreads + deep:
        g.wait_send()

    def finish_gather(c, _):
        forward(c).wait_send()
        return 0

    lax.fori_loop(0, NX * NY, finish_gather, 0)

    def finish(xs, _):
        for d in (0, 1):
            for s in (1, 2, 3, 4):
                rs_data(d, xs, s).wait_send()
                rs_bound(d, xs, s).wait_send()
                ag(d, xs, s).wait_send()
        return 0

    lax.fori_loop(0, NX, finish, 0)

    def finish_out(o, _):
        out_copy(o).wait()
        return 0

    lax.fori_loop(0, NZ, finish_out, 0)


def local(hidden, labels, head_weight, hess_old):
    dma = pltpu.SemaphoreType.DMA
    return pl.pallas_call(
        kernel,
        out_shape=jax.ShapeDtypeStruct(hess_old.shape, BF16),
        in_specs=[pl.BlockSpec(memory_space=pl.ANY)] * 4,
        out_specs=pl.BlockSpec(memory_space=pl.ANY),
        scratch_shapes=[
            pltpu.VMEM((NZ * OWN, WIDTH), BF16),
            pltpu.VMEM((NZ * OWN, WIDTH), BF16),
            pltpu.VMEM((TOK, WIDTH), BF16),
            pltpu.VMEM((NZ, 1, 128), jnp.int32),
            pltpu.VMEM((NX, NZ, OWN, SB), F32),
            pltpu.VMEM((NX, NZ, 2, SB), F32),
            pltpu.VMEM((2, NX, 4, OWN, SB), I16),
            pltpu.VMEM((2, NX, HALF, SB), I16),
            pltpu.VMEM((2, NX, 5, 2, SB), F32),
            pltpu.VMEM((NZ, NX, OWN, SB), I16),
            pltpu.VMEM((16, 128), F32),
            pltpu.VMEM((16, 128), F32),
            pltpu.VMEM((NX * NY, 16, 128), F32),
            pltpu.VMEM((NZ, 24, 128), F32),
            pltpu.VMEM((16, 128), F32),
            pltpu.VMEM((OWN, TOK), BF16),
            pltpu.VMEM((NZ * OWN, WIDTH), BF16),
            dma((3,)),
            dma((15,)), dma((16,)), dma((16,)), dma((16,)),
            dma((7,)), dma((7,)),
            dma((2, NX, 4)), dma((2, NX, 4)),
            dma((2, NX, 4)), dma((2, NX, 4)),
            dma((2, NX, 4)), dma((2, NX, 4)),
            dma((15,)), dma((16,)),
            dma, dma,
            dma((7,)), dma((7,)),
            dma((NZ,)),
        ],
        compiler_params=pltpu.CompilerParams(
            collective_id=0, has_side_effects=True, vmem_limit_bytes=56 * 2**20
        ),
        cost_estimate=pl.CostEstimate(
            flops=8 * TOK * NZ * OWN * WIDTH, bytes_accessed=13 * 2**20, transcendentals=TOK * NZ * OWN
        ),
    )(hidden, labels.reshape(1, 128), head_weight, hess_old)


def solution(mesh):
    in_specs = (P("vocab", "dp"), P("dp"), P("vocab", "dp"), P("vocab", "dp"))
    out_specs = P("vocab", "dp")
    return jax.shard_map(local, mesh=mesh, in_specs=in_specs, out_specs=out_specs, check_vma=False)
```

```python
import functools

import jax
import jax.numpy as jnp
from jax import lax
from jax.experimental import pallas as pl
from jax.experimental.pallas import tpu as pltpu
from jax.sharding import PartitionSpec as P

MESH = pl.DeviceIdType.MESH
F32, BF16, I16 = jnp.float32, jnp.bfloat16, jnp.int16
NZ, NX, NY = 8, 4, 4
OWN = 256
HALF = 128
SB = 256
TOK = 1024
WIDTH = 1024
BLK = 32
TOP = 32760.0
TINY = 1e-30
SLOTS = (
    (0, 0), (0, 1), (0, 3), (1, 0),
    (3, 0), (1, 1), (3, 3), (1, 3),
    (3, 1), (2, 0), (0, 2), (2, 1),
    (2, 3), (1, 2), (3, 2), (2, 2),
)
HOPS = {
    0: ((1, (0, 1)), (2, (0, 3)), (3, (1, 0)), (4, (3, 0))),
    1: ((8, (3, 0)), (10, (0, 1))),
    2: ((7, (1, 0)),),
    3: ((5, (0, 1)), (9, (1, 0))),
    4: ((6, (0, 3)),),
    5: ((11, (1, 0)),),
    6: ((12, (3, 0)),),
    7: ((13, (0, 3)),),
    8: ((14, (0, 1)),),
    14: ((15, (3, 0)),),
}
ARRIVE = ((1, 2, 3, 4), (5, 6, 7, 8, 9, 10), (11, 12, 13, 14), (15,))
ORDER = ((1, 0), (1, 1), (2, 0), (1, 2), (2, 1), (1, 3), (2, 2), (3, 0), (2, 3), (3, 1), (3, 2), (3, 3))


def pick(k, values):
    out = values[0]
    for j in range(1, len(values)):
        out = jnp.where(k == j, values[j], out)
    return out


def kernel(
    hid_ref, lab_ref, w_ref, hess_ref, out_ref,
    w_v, hess_v, h_v, lab_v, lab_t, lab_l, part, mb, rb, rf, bb, lg, st_l, st, st_f, st_sib, st_y, st_x, st_z, stat, res,
    loc_sem, g_send, g_recv, f_send, f_recv, lab_send, lab_recv, rs_send, rs_recv, bs_send, bs_recv,
    ag_send, ag_recv, sy_send, sy_recv, sx_send, sx_recv, sib_send, sib_recv, sz_send, sz_recv,
):
    z = lax.axis_index("dp")
    v = lax.axis_index("vocab")
    core = lax.rem(v, 2)
    chip = v // 2
    x, y = chip // NY, lax.rem(chip, NY)
    sib = (z, v + 1 - 2 * core)

    def zmod(a):
        return lax.rem(a + 2 * NZ, NZ)

    def at(dx, dy):
        return (z, (lax.rem(x + dx, NX) * NY + lax.rem(y + dy, NY)) * 2 + core)

    def chip_of(k):
        dx, dy = SLOTS[k]
        return lax.rem(x + NX - dx, NX) * NY + lax.rem(y + NY - dy, NY)

    def remote(src, dst, ssem, rsem, dev):
        return pltpu.make_async_remote_copy(
            src_ref=src, dst_ref=dst, send_sem=ssem, recv_sem=rsem, device_id=dev, device_id_type=MESH
        )

    w_copy = pltpu.make_async_copy(w_ref, w_v, loc_sem.at[0])
    hess_copy = pltpu.make_async_copy(hess_ref, hess_v, loc_sem.at[1])
    lab_copy = pltpu.make_async_copy(lab_ref, lab_v.at[z], loc_sem.at[2])

    def slot(k, co):
        return h_v.at[pl.ds(pl.multiple_of(k * 2 * BLK + co * BLK, BLK), BLK)]

    own_copy = pltpu.make_async_copy(hid_ref, slot(0, core), loc_sem.at[3])
    w_copy.start()
    lab_copy.start()
    own_copy.start()

    zring = ((zmod(z + 1), v), (zmod(z - 1), v))
    zpeers = [(zmod(z + k), v) for k in range(1, NZ)]
    ypeers = [at(0, d) for d in range(1, NY)]
    xpeers = [at(d, 0) for d in range(1, NX)]

    barrier = pltpu.get_barrier_semaphore()
    partners = zpeers + ypeers + xpeers + [sib]
    for dev in partners:
        pl.semaphore_signal(barrier, inc=1, device_id=dev, device_id_type=MESH)
    pl.semaphore_wait(barrier, len(partners))

    def hop(k, c, step):
        src = hid_ref if k == 0 else slot(k, core)
        return remote(src, slot(c, core), g_send.at[c], g_recv.at[c], at(*step))

    def share(k):
        src = hid_ref if k == 0 else slot(k, core)
        return remote(src, slot(k, core), f_send.at[k], f_recv.at[k], sib)

    for c, step in HOPS[0]:
        hop(0, c, step).start()
    share(0).start()
    labs = [
        remote(lab_ref, lab_v.at[z], lab_send.at[k], lab_recv.at[k], dev) for k, dev in enumerate(zpeers)
    ]
    for g in labs:
        g.start()
    hess_copy.start()
    own_copy.wait()
    w_copy.wait()

    def gather_group(i):
        for k in ARRIVE[i]:
            remote(slot(k, core), slot(k, core), g_send.at[k], g_recv.at[k], sib).wait_recv()
            for c, step in HOPS.get(k, ()):
                hop(k, c, step).start()
            share(k).start()
        for k in range(4 * i, 4 * i + 4):
            remote(slot(k, 1 - core), slot(k, 1 - core), f_send.at[k], f_recv.at[k], sib).wait_recv()

    def mm(xs, o):
        a = w_v[pl.ds(pl.multiple_of(o * OWN, OWN), OWN), :]
        b = h_v[pl.ds(pl.multiple_of(xs * SB, SB), SB), :]
        p = lax.dot_general(a, b, (((1,), (1,)), ((), ())), preferred_element_type=F32)
        part[xs, o] = p
        mb[xs, o, 0:1, :] = jnp.max(jnp.abs(p[:HALF]), axis=0, keepdims=True)
        mb[xs, o, 1:2, :] = jnp.max(jnp.abs(p[HALF:]), axis=0, keepdims=True)

    def rows_of(xs, o, half):
        return part[xs, o, half * HALF : (half + 1) * HALF, :]

    def to_int(q):
        return jnp.round(q).astype(I16)

    def first(d, xs, place, o, half):
        b = mb[xs, o, half : half + 1, :]
        scale = TOP / jnp.maximum(b, TINY)
        rb[d, xs, 0, place * HALF : (place + 1) * HALF, :] = to_int(rows_of(xs, o, half) * scale)
        bb[d, xs, 0, place : place + 1, :] = b

    def fold(d, xs, slot, place, o, half):
        b_in = bb[d, xs, slot, place : place + 1, :]
        b = b_in + mb[xs, o, half : half + 1, :]
        inv = 1.0 / jnp.maximum(b, TINY)
        got = rb[d, xs, slot, place * HALF : (place + 1) * HALF, :].astype(F32)
        q = got * (b_in * inv) + rows_of(xs, o, half) * (TOP * inv)
        rb[d, xs, slot, place * HALF : (place + 1) * HALF, :] = to_int(q)
        bb[d, xs, slot, place : place + 1, :] = b

    def rs_data(d, xs, s):
        if not isinstance(s, int) or s < 4:
            src, dst = rb.at[d, xs, s - 1], rb.at[d, xs, s]
        else:
            src, dst = rb.at[d, xs, 3, pl.ds(0, HALF)], rf.at[d, xs]
        return remote(src, dst, rs_send.at[d, xs, s - 1], rs_recv.at[d, xs, s - 1], zring[d])

    def rs_bound(d, xs, s):
        return remote(
            bb.at[d, xs, s - 1], bb.at[d, xs, s], bs_send.at[d, xs, s - 1], bs_recv.at[d, xs, s - 1], zring[d]
        )

    def rs_start(d, xs, s):
        rs_bound(d, xs, s).start()
        rs_data(d, xs, s).start()

    def rs_wait(d, xs, s):
        rs_bound(d, xs, s).wait_recv()
        rs_data(d, xs, s).wait_recv()

    def event(k, _):
        s = pick(k, [e[0] for e in ORDER])
        i = pick(k, [e[1] for e in ORDER])

        for g in range(4):

            @pl.when((s == 1) & (i == g))
            def _(g=g):
                gather_group(g)

        @pl.when(s == 1)
        def _():
            def owners(j, _):
                mm(i, zmod(z + 3 + j))
                return 0

            lax.fori_loop(0, 3, owners, 0)
            first(0, i, 0, zmod(z + 4), 0)
            first(0, i, 1, zmod(z + 3), 1)
            rs_start(0, i, 1)
            first(1, i, 0, zmod(z - 4), 1)
            first(1, i, 1, zmod(z - 3), 0)
            rs_start(1, i, 1)

        @pl.when(s > 1)
        def _():
            def owners(j, _):
                mm(i, zmod(z + (4 - s) * (1 - 2 * j)))
                return 0

            lax.fori_loop(0, 2, owners, 0)
            rs_wait(0, i, s - 1)
            fold(0, i, s - 1, 0, zmod(z + 5 - s), 0)
            fold(0, i, s - 1, 1, zmod(z + 4 - s), 1)
            rs_start(0, i, s)
            rs_wait(1, i, s - 1)
            fold(1, i, s - 1, 0, zmod(z - 5 + s), 1)
            fold(1, i, s - 1, 1, zmod(z - 4 + s), 0)
            rs_start(1, i, s)

        return 0

    lax.fori_loop(0, len(ORDER), event, 0)

    def step4(i, _):
        xs = i
        rs_wait(0, xs, 3)
        fold(0, xs, 3, 0, zmod(z + 1), 0)
        rs_start(0, xs, 4)
        rs_wait(1, xs, 3)
        fold(1, xs, 3, 0, zmod(z - 1), 1)
        rs_start(1, xs, 4)
        mm(xs, z)
        return 0

    lax.fori_loop(0, NX, step4, 0)

    def ag(d, xs, s):
        o = zmod(z + 1 - s) if d == 0 else zmod(z - 1 + s)
        ref = lg.at[o, xs]
        if s == 4:
            ref = lg.at[o, xs, pl.ds(d * HALF, HALF)]
        return remote(ref, ref, ag_send.at[d, xs, s - 1], ag_recv.at[d, xs, s - 1], zring[d])

    def ag_wait(d, xs, s):
        o = zmod(z - s) if d == 0 else zmod(z + s)
        ref = lg.at[o, xs]
        if s == 4:
            ref = lg.at[o, xs, pl.ds(d * HALF, HALF)]
        remote(ref, ref, ag_send.at[d, xs, s - 1], ag_recv.at[d, xs, s - 1], zring[d]).wait_recv()

    def total(i, _):
        xs = i
        rs_wait(0, xs, 4)
        rs_wait(1, xs, 4)
        b0, b1 = bb[0, xs, 4, 0:1, :], bb[1, xs, 3, 1:2, :]
        c0, c1 = bb[1, xs, 4, 0:1, :], bb[0, xs, 3, 1:2, :]
        k = 1.0 / TOP
        upper = rows_of(xs, z, 0) + rf[0, xs].astype(F32) * (b0 * k) + rb[1, xs, 3, HALF:, :].astype(F32) * (b1 * k)
        lower = rows_of(xs, z, 1) + rf[1, xs].astype(F32) * (c0 * k) + rb[0, xs, 3, HALF:, :].astype(F32) * (c1 * k)
        b = jnp.maximum(mb[xs, z, 0:1, :] + b0 + b1, mb[xs, z, 1:2, :] + c0 + c1)
        b = jnp.maximum(b, TINY)
        scale = TOP / b
        lg[z, xs, :HALF, :] = to_int(upper * scale)
        lg[z, xs, HALF:, :] = to_int(lower * scale)
        ag(0, xs, 1).start()
        ag(1, xs, 1).start()
        m = jnp.maximum(jnp.max(upper, axis=0, keepdims=True), jnp.max(lower, axis=0, keepdims=True))
        e = jnp.sum(jnp.exp(upper - m), axis=0, keepdims=True) + jnp.sum(jnp.exp(lower - m), axis=0, keepdims=True)
        for j in range(2):
            lanes = slice(128 * j, 128 * (j + 1))
            st_l[pl.ds(2 * xs + j, 1), :] = m[:, lanes]
            st_l[pl.ds(8 + 2 * xs + j, 1), :] = e[:, lanes]
            st_z[z, pl.ds(16 + 2 * xs + j, 1), :] = b[:, lanes] * k
        return 0

    lax.fori_loop(0, NX, total, 0)

    left8 = lax.broadcasted_iota(jnp.int32, (8, 128), 1) < 64
    left16 = lax.broadcasted_iota(jnp.int32, (16, 128), 1) < 64

    def swap(a):
        return pltpu.roll(a, 64, 1)

    def merge(parts):
        m = parts[0]
        for a in parts[1:]:
            m = jnp.maximum(m, a)
        e = jnp.zeros_like(m)
        for a in parts:
            e = e + a * swap(jnp.exp(a - m))
        return jnp.where(left16, m, e)

    m, e = st_l[0:8], st_l[8:16]
    even, odd = jnp.where(left8, m, swap(e)), jnp.where(left8, swap(m), e)
    for r in range(8):
        st[pl.ds(chip_of(2 * r), 1), :] = even[r : r + 1]
        st[pl.ds(chip_of(2 * r + 1), 1), :] = odd[r : r + 1]

    sib_copy = remote(st, st_sib, sib_send, sib_recv, sib)
    ycopies = [remote(st_y.at[0], st_y.at[d], sy_send.at[d], sy_recv.at[d], ypeers[d - 1]) for d in range(1, NY)]
    xcopies = [remote(st_x.at[0], st_x.at[d], sx_send.at[d], sx_recv.at[d], xpeers[d - 1]) for d in range(1, NX)]
    zcopies = [remote(st_z.at[z], st_z.at[z], sz_send.at[k], sz_recv.at[k], dev) for k, dev in enumerate(zpeers)]
    sib_copy.start()
    sib_copy.wait_recv()
    st_y[0] = merge([st[...], st_sib[...]])
    for g in ycopies:
        g.start()

    def ag_next(i, s):
        for d in (0, 1):
            ag_wait(d, i, s - 1)
            ag(d, i, s).start()

    def ag_two(i, _):
        ag_next(i, 2)

        @pl.when(i == 1)
        def _():
            for g in ycopies:
                g.wait_recv()
            st_x[0] = merge([st_y[d] for d in range(NY)])
            for g in xcopies:
                g.start()

        @pl.when(i == 3)
        def _():
            for g in xcopies:
                g.wait_recv()
            st_z[z, 0:16] = merge([st_x[d] for d in range(NX)])
            for g in zcopies:
                g.start()

        return 0

    lax.fori_loop(0, NX, ag_two, 0)

    def settle():
        for k in range(NZ - 1):
            o = zmod(z - 1 - k)
            remote(st_z.at[o], st_z.at[o], sz_send.at[k], sz_recv.at[k], sib).wait_recv()
            remote(lab_v.at[o], lab_v.at[o], lab_send.at[k], lab_recv.at[k], sib).wait_recv()
        lab_copy.wait()
        hess_copy.wait()
        st_f[...] = merge([st_z[o, 0:16] for o in range(NZ)])
        for r in range(8):
            lab_t[r : r + 1, :] = lab_v[r]
        lab_t[8:16] = swap(lab_t[0:8])
        for r in range(8):
            a, b = chip_of(2 * r), chip_of(2 * r + 1)
            st_l[r : r + 1, :] = st_f[pl.ds(a, 1), :]
            st_l[8 + r : 9 + r, :] = st_f[pl.ds(b, 1), :]
            lab_l[r : r + 1, :] = jnp.where(
                left8[0:1], lab_t[pl.ds(a // 2 + 8 * lax.rem(a, 2), 1), :], lab_t[pl.ds(b // 2 + 8 * (1 - lax.rem(b, 2)), 1), :]
            )
        a, b = st_l[0:8], st_l[8:16]
        stat[0:8] = jnp.where(left8, a, swap(b))
        stat[8:16] = 1.0 / jnp.where(left8, swap(a), b)

    def prep(o, i):
        base = v * (NZ * OWN) + o * OWN
        for h in range(2):
            r = 2 * i + h
            top, inv = stat[pl.ds(r, 1), :], stat[pl.ds(8 + r, 1), :]
            scale = st_z[o, pl.ds(16 + r, 1), :]
            lab = lab_l[pl.ds(r, 1), :]
            for q in range(4):
                sub = slice(64 * q, 64 * (q + 1))
                l = lg[o, i, sub, 128 * h : 128 * (h + 1)].astype(F32) * scale
                p = jnp.exp(l - top) * inv
                ids = base + 64 * q + lax.broadcasted_iota(jnp.int32, (64, 128), 0)
                lanes = pl.ds(pl.multiple_of(256 * i + 128 * h, 128), 128)
                res[sub, lanes] = (p - (ids == lab).astype(F32)).astype(BF16)

    def tile(o, n):
        cols = pl.ds(pl.multiple_of(n * 256, 256), 256)
        sums = jnp.dot(res[...], h_v[:, cols], preferred_element_type=F32)
        rws = pl.ds(pl.multiple_of(o * OWN, OWN), OWN)
        fresh = 0.9 * hess_v[rws, cols].astype(F32) + 0.1 * sums * sums
        out_ref[rws, cols] = jnp.clip(sums / (10000.0 * fresh), -1.0, 1.0).astype(BF16)

    def last(k, _):
        @pl.when(k < NX)
        def _():
            ag_next(k, 3)

        @pl.when(k == 0)
        def _():
            settle()

        @pl.when((k >= NX) & (k < 2 * NX))
        def _():
            ag_next(k - NX, 4)

        u = jnp.where(k < 6, k - 1, k - 3)
        o = zmod(z + ((u + 1) // 2) * (1 - 2 * lax.rem(u + 2, 2)))

        @pl.when(((k >= 1) & (k < 6)) | (k >= 8))
        def _():
            def preps(i, _):
                @pl.when(k == 10)
                def _():
                    for d in (0, 1):
                        ag_wait(d, i, 4)

                prep(o, i)
                return 0

            lax.fori_loop(0, NX, preps, 0)

            def tiles(n, _):
                tile(o, n)
                return 0

            lax.fori_loop(0, WIDTH // 256, tiles, 0)

        return 0

    lax.fori_loop(0, 11, last, 0)

    for c in range(1, 16):
        remote(slot(c, core), slot(c, core), g_send.at[c], g_recv.at[c], sib).wait_send()
    for k in range(16):
        share(k).wait_send()
    for g in labs + [sib_copy] + ycopies + xcopies + zcopies:
        g.wait_send()

    def finish(xs, _):
        for d in (0, 1):
            for s in (1, 2, 3, 4):
                rs_data(d, xs, s).wait_send()
                rs_bound(d, xs, s).wait_send()
                ag(d, xs, s).wait_send()
        return 0

    lax.fori_loop(0, NX, finish, 0)


def local(hidden, labels, head_weight, hess_old):
    dma = pltpu.SemaphoreType.DMA
    return pl.pallas_call(
        kernel,
        out_shape=pltpu.VMEM(hess_old.shape, BF16),
        in_specs=[pl.BlockSpec(memory_space=pl.ANY)] * 4,
        out_specs=pl.BlockSpec(memory_space=pltpu.VMEM),
        scratch_shapes=[
            pltpu.VMEM((NZ * OWN, WIDTH), BF16),
            pltpu.VMEM((NZ * OWN, WIDTH), BF16),
            pltpu.VMEM((TOK, WIDTH), BF16),
            pltpu.VMEM((NZ, 1, 128), jnp.int32),
            pltpu.VMEM((16, 128), jnp.int32),
            pltpu.VMEM((8, 128), jnp.int32),
            pltpu.VMEM((NX, NZ, OWN, SB), F32),
            pltpu.VMEM((NX, NZ, 2, SB), F32),
            pltpu.VMEM((2, NX, 4, OWN, SB), I16),
            pltpu.VMEM((2, NX, HALF, SB), I16),
            pltpu.VMEM((2, NX, 5, 2, SB), F32),
            pltpu.VMEM((NZ, NX, OWN, SB), I16),
            pltpu.VMEM((16, 128), F32),
            pltpu.VMEM((16, 128), F32),
            pltpu.VMEM((16, 128), F32),
            pltpu.VMEM((16, 128), F32),
            pltpu.VMEM((NY, 16, 128), F32),
            pltpu.VMEM((NX, 16, 128), F32),
            pltpu.VMEM((NZ, 24, 128), F32),
            pltpu.VMEM((16, 128), F32),
            pltpu.VMEM((OWN, TOK), BF16),
            dma((4,)),
            dma((16,)), dma((16,)), dma((16,)), dma((16,)),
            dma((7,)), dma((7,)),
            dma((2, NX, 4)), dma((2, NX, 4)),
            dma((2, NX, 4)), dma((2, NX, 4)),
            dma((2, NX, 4)), dma((2, NX, 4)),
            dma((NY,)), dma((NY,)),
            dma((NX,)), dma((NX,)),
            dma, dma,
            dma((7,)), dma((7,)),
        ],
        compiler_params=pltpu.CompilerParams(
            collective_id=0, has_side_effects=True, vmem_limit_bytes=56 * 2**20
        ),
        cost_estimate=pl.CostEstimate(
            flops=8 * TOK * NZ * OWN * WIDTH, bytes_accessed=13 * 2**20, transcendentals=TOK * NZ * OWN
        ),
    )(hidden, labels.reshape(1, 128), head_weight, hess_old)


def solution(mesh):
    in_specs = (P("vocab", "dp"), P("dp"), P("vocab", "dp"), P("vocab", "dp"))
    out_specs = P("vocab", "dp")
    return jax.shard_map(local, mesh=mesh, in_specs=in_specs, out_specs=out_specs, check_vma=False)
```

```python
import functools

import jax
import jax.numpy as jnp
from jax import lax
from jax.experimental import pallas as pl
from jax.experimental.pallas import tpu as pltpu
from jax.sharding import PartitionSpec as P

MESH = pl.DeviceIdType.MESH
F32, BF16, I16 = jnp.float32, jnp.bfloat16, jnp.int16
NZ, NX, NY = 8, 4, 4
OWN = 256
HALF = 128
SB = 256
TOK = 1024
WIDTH = 1024
BLK = 32
TOP = 32760.0
TINY = 1e-30
SLOTS = (
    (0, 0), (0, 1), (0, 3), (1, 0),
    (3, 0), (1, 1), (3, 3), (1, 3),
    (3, 1), (2, 0), (0, 2), (2, 1),
    (2, 3), (1, 2), (3, 2), (2, 2),
)
HOPS = {
    0: (
        (1, (0, 1)), (2, (0, 3)), (3, (1, 0)), (4, (3, 0)),
        (5, (1, 1)), (6, (3, 3)), (7, (1, 3)), (8, (3, 1)),
    ),
    1: ((10, (0, 1)),),
    3: ((9, (1, 0)),),
    5: ((11, (1, 0)),),
    6: ((12, (3, 0)),),
    7: ((13, (0, 3)),),
    8: ((14, (0, 1)),),
    14: ((15, (3, 0)),),
}
ARRIVE = ((1, 2, 3, 4), (5, 6, 7, 8), (9, 10, 11, 12, 13, 14), (15,))
ORDER = ((1, 0), (1, 1), (2, 0), (1, 2), (2, 1), (1, 3), (2, 2), (3, 0), (2, 3), (3, 1), (3, 2), (3, 3))


def pick(k, values):
    out = values[0]
    for j in range(1, len(values)):
        out = jnp.where(k == j, values[j], out)
    return out


def step_of(sums, old):
    fresh = 0.9 * old.astype(F32) + 0.1 * sums * sums
    return jnp.clip(sums / (10000.0 * fresh), -1.0, 1.0).astype(BF16)


def kernel(
    hid_ref, lab_ref, w_ref, hess_ref, out_ref, res, h_v, hess_l,
    w_v, hess_v, lab_v, lab_t, lab_l, part, mb, rb, rf, bb, lg, st_l, st, st_f, st_sib, st_y, st_x, st_z, stat,
    loc_sem, g_send, g_recv, f_send, f_recv, lab_send, lab_recv, rs_send, rs_recv, bs_send, bs_recv,
    ag_send, ag_recv, sy_send, sy_recv, sx_send, sx_recv, sib_send, sib_recv, sz_send, sz_recv,
):
    z = lax.axis_index("dp")
    v = lax.axis_index("vocab")
    core = lax.rem(v, 2)
    chip = v // 2
    x, y = chip // NY, lax.rem(chip, NY)
    sib = (z, v + 1 - 2 * core)

    def zmod(a):
        return lax.rem(a + 2 * NZ, NZ)

    def at(dx, dy):
        return (z, (lax.rem(x + dx, NX) * NY + lax.rem(y + dy, NY)) * 2 + core)

    def chip_of(k):
        dx, dy = SLOTS[k]
        return lax.rem(x + NX - dx, NX) * NY + lax.rem(y + NY - dy, NY)

    def remote(src, dst, ssem, rsem, dev):
        return pltpu.make_async_remote_copy(
            src_ref=src, dst_ref=dst, send_sem=ssem, recv_sem=rsem, device_id=dev, device_id_type=MESH
        )

    w_copy = pltpu.make_async_copy(w_ref, w_v, loc_sem.at[0])
    hess_copy = pltpu.make_async_copy(hess_ref, hess_v, loc_sem.at[1])
    lab_copy = pltpu.make_async_copy(lab_ref, lab_v.at[z], loc_sem.at[2])

    def slot(k, co):
        return h_v.at[pl.ds(pl.multiple_of(k * 2 * BLK + co * BLK, BLK), BLK)]

    far = pl.ds(pl.multiple_of(zmod(z + 4) * OWN, OWN), OWN)
    far_copy = pltpu.make_async_copy(hess_ref.at[far], hess_l, loc_sem.at[4])
    own_copy = pltpu.make_async_copy(hid_ref, slot(0, core), loc_sem.at[3])
    w_copy.start()
    lab_copy.start()
    own_copy.start()

    zring = ((zmod(z + 1), v), (zmod(z - 1), v))
    zpeers = [(zmod(z + k), v) for k in range(1, NZ)]
    ypeers = [at(0, d) for d in range(1, NY)]
    xpeers = [at(d, 0) for d in range(1, NX)]

    barrier = pltpu.get_barrier_semaphore()
    partners = list(zring) + [at(0, 1), at(0, 3), at(1, 0), at(3, 0), sib]
    partners += [at(dx, dy) for dx in (1, 3) for dy in (1, 3)]
    for dev in partners:
        pl.semaphore_signal(barrier, inc=1, device_id=dev, device_id_type=MESH)
    pl.semaphore_wait(barrier, len(partners))

    def hop(k, c, step):
        src = hid_ref if k == 0 else slot(k, core)
        return remote(src, slot(c, core), g_send.at[c], g_recv.at[c], at(*step))

    def share(k):
        src = hid_ref if k == 0 else slot(k, core)
        return remote(src, slot(k, core), f_send.at[k], f_recv.at[k], sib)

    for c, step in HOPS[0][:4]:
        hop(0, c, step).start()
    share(0).start()
    def lab_hop(d, step):
        o = zmod(z + 1 - step) if d == 0 else zmod(z - 1 + step)
        return remote(lab_v.at[o], lab_v.at[o], lab_send.at[d, step - 1], lab_recv.at[d, step - 1], zring[d])

    lab_copy.wait()
    for d in (0, 1):
        lab_hop(d, 1).start()
    own_copy.wait()
    w_copy.wait()
    for c, step in HOPS[0][:4]:
        hop(0, c, step).wait_send()
    for c, step in HOPS[0][4:]:
        hop(0, c, step).start()

    def gather_group(i):
        for k in ARRIVE[i]:
            remote(slot(k, core), slot(k, core), g_send.at[k], g_recv.at[k], sib).wait_recv()
            for c, step in HOPS.get(k, ()):
                hop(k, c, step).start()
            share(k).start()
        for k in range(4 * i, 4 * i + 4):
            remote(slot(k, 1 - core), slot(k, 1 - core), f_send.at[k], f_recv.at[k], sib).wait_recv()

    def mm(xs, o):
        a = w_v[pl.ds(pl.multiple_of(o * OWN, OWN), OWN), :]
        b = h_v[pl.ds(pl.multiple_of(xs * SB, SB), SB), :]
        p = lax.dot_general(a, b, (((1,), (1,)), ((), ())), preferred_element_type=F32)
        part[xs, o] = p
        mb[xs, o, 0:1, :] = jnp.max(jnp.abs(p[:HALF]), axis=0, keepdims=True)
        mb[xs, o, 1:2, :] = jnp.max(jnp.abs(p[HALF:]), axis=0, keepdims=True)

    def rows_of(xs, o, half):
        return part[xs, o, half * HALF : (half + 1) * HALF, :]

    def to_int(q):
        return jnp.round(q).astype(I16)

    def first(d, xs, place, o, half):
        b = mb[xs, o, half : half + 1, :]
        scale = TOP / jnp.maximum(b, TINY)
        rb[d, xs, 0, place * HALF : (place + 1) * HALF, :] = to_int(rows_of(xs, o, half) * scale)
        bb[d, xs, 0, place : place + 1, :] = b

    def fold(d, xs, slot, place, o, half):
        b_in = bb[d, xs, slot, place : place + 1, :]
        b = b_in + mb[xs, o, half : half + 1, :]
        inv = 1.0 / jnp.maximum(b, TINY)
        got = rb[d, xs, slot, place * HALF : (place + 1) * HALF, :].astype(F32)
        q = got * (b_in * inv) + rows_of(xs, o, half) * (TOP * inv)
        rb[d, xs, slot, place * HALF : (place + 1) * HALF, :] = to_int(q)
        bb[d, xs, slot, place : place + 1, :] = b

    def rs_data(d, xs, s):
        if not isinstance(s, int) or s < 4:
            src, dst = rb.at[d, xs, s - 1], rb.at[d, xs, s]
        else:
            src, dst = rb.at[d, xs, 3, pl.ds(0, HALF)], rf.at[d, xs]
        return remote(src, dst, rs_send.at[d, xs, s - 1], rs_recv.at[d, xs, s - 1], zring[d])

    def rs_bound(d, xs, s):
        return remote(
            bb.at[d, xs, s - 1], bb.at[d, xs, s], bs_send.at[d, xs, s - 1], bs_recv.at[d, xs, s - 1], zring[d]
        )

    def rs_start(d, xs, s):
        rs_bound(d, xs, s).start()
        rs_data(d, xs, s).start()

    def rs_wait(d, xs, s):
        rs_bound(d, xs, s).wait_recv()
        rs_data(d, xs, s).wait_recv()

    def event(k, _):
        s = pick(k, [e[0] for e in ORDER])
        i = pick(k, [e[1] for e in ORDER])

        for g in range(4):

            @pl.when((s == 1) & (i == g))
            def _(g=g):
                gather_group(g)

        @pl.when(s == 1)
        def _():
            def owners(j, _):
                mm(i, zmod(z + 3 + j))
                return 0

            lax.fori_loop(0, 2, owners, 0)
            first(0, i, 0, zmod(z + 4), 0)
            first(0, i, 1, zmod(z + 3), 1)
            rs_start(0, i, 1)
            lax.fori_loop(2, 3, owners, 0)
            first(1, i, 0, zmod(z - 4), 1)
            first(1, i, 1, zmod(z - 3), 0)
            rs_start(1, i, 1)

        @pl.when(s > 1)
        def _():
            def owners(j, _):
                mm(i, zmod(z + (4 - s) * (1 - 2 * j)))
                return 0

            lax.fori_loop(0, 2, owners, 0)
            rs_wait(0, i, s - 1)
            fold(0, i, s - 1, 0, zmod(z + 5 - s), 0)
            fold(0, i, s - 1, 1, zmod(z + 4 - s), 1)
            rs_start(0, i, s)
            rs_wait(1, i, s - 1)
            fold(1, i, s - 1, 0, zmod(z - 5 + s), 1)
            fold(1, i, s - 1, 1, zmod(z - 4 + s), 0)
            rs_start(1, i, s)

        for step in (1, 2, 3):

            @pl.when(k == 3 * step)
            def _(step=step):
                for d in (0, 1):
                    lab_hop(d, step).wait_recv()
                    if step < 3 or d == 0:
                        lab_hop(d, step + 1).start()

        return 0

    lax.fori_loop(0, len(ORDER), event, 0)

    hess_copy.start()
    far_copy.start()

    def step4(i, _):
        xs = i
        rs_wait(0, xs, 3)
        fold(0, xs, 3, 0, zmod(z + 1), 0)
        rs_start(0, xs, 4)
        rs_wait(1, xs, 3)
        fold(1, xs, 3, 0, zmod(z - 1), 1)
        rs_start(1, xs, 4)
        mm(xs, z)
        return 0

    lax.fori_loop(0, NX, step4, 0)

    def ag(d, xs, s):
        o = zmod(z + 1 - s) if d == 0 else zmod(z - 1 + s)
        ref = lg.at[o, xs]
        if s == 4:
            ref = lg.at[o, xs, pl.ds(d * HALF, HALF)]
        return remote(ref, ref, ag_send.at[d, xs, s - 1], ag_recv.at[d, xs, s - 1], zring[d])

    def ag_wait(d, xs, s):
        o = zmod(z - s) if d == 0 else zmod(z + s)
        ref = lg.at[o, xs]
        if s == 4:
            ref = lg.at[o, xs, pl.ds(d * HALF, HALF)]
        remote(ref, ref, ag_send.at[d, xs, s - 1], ag_recv.at[d, xs, s - 1], zring[d]).wait_recv()

    def total(i, _):
        xs = i
        rs_wait(0, xs, 4)
        rs_wait(1, xs, 4)
        b0, b1 = bb[0, xs, 4, 0:1, :], bb[1, xs, 3, 1:2, :]
        c0, c1 = bb[1, xs, 4, 0:1, :], bb[0, xs, 3, 1:2, :]
        k = 1.0 / TOP
        upper = rows_of(xs, z, 0) + rf[0, xs].astype(F32) * (b0 * k) + rb[1, xs, 3, HALF:, :].astype(F32) * (b1 * k)
        lower = rows_of(xs, z, 1) + rf[1, xs].astype(F32) * (c0 * k) + rb[0, xs, 3, HALF:, :].astype(F32) * (c1 * k)
        b = jnp.maximum(mb[xs, z, 0:1, :] + b0 + b1, mb[xs, z, 1:2, :] + c0 + c1)
        b = jnp.maximum(b, TINY)
        scale = TOP / b
        lg[z, xs, :HALF, :] = to_int(upper * scale)
        lg[z, xs, HALF:, :] = to_int(lower * scale)
        ag(0, xs, 1).start()
        ag(1, xs, 1).start()
        m = jnp.maximum(jnp.max(upper, axis=0, keepdims=True), jnp.max(lower, axis=0, keepdims=True))
        e = jnp.sum(jnp.exp(upper - m), axis=0, keepdims=True) + jnp.sum(jnp.exp(lower - m), axis=0, keepdims=True)
        for j in range(2):
            lanes = slice(128 * j, 128 * (j + 1))
            st_l[pl.ds(2 * xs + j, 1), :] = m[:, lanes]
            st_l[pl.ds(8 + 2 * xs + j, 1), :] = e[:, lanes]
            st_z[z, pl.ds(16 + 2 * xs + j, 1), :] = b[:, lanes] * k
        return 0

    lax.fori_loop(0, NX, total, 0)

    left8 = lax.broadcasted_iota(jnp.int32, (8, 128), 1) < 64
    left16 = lax.broadcasted_iota(jnp.int32, (16, 128), 1) < 64

    def swap(a):
        return pltpu.roll(a, 64, 1)

    def merge(parts):
        m = parts[0]
        for a in parts[1:]:
            m = jnp.maximum(m, a)
        e = jnp.zeros_like(m)
        for a in parts:
            e = e + a * swap(jnp.exp(a - m))
        return jnp.where(left16, m, e)

    m, e = st_l[0:8], st_l[8:16]
    even, odd = jnp.where(left8, m, swap(e)), jnp.where(left8, swap(m), e)
    for r in range(8):
        st[pl.ds(chip_of(2 * r), 1), :] = even[r : r + 1]
        st[pl.ds(chip_of(2 * r + 1), 1), :] = odd[r : r + 1]

    sib_copy = remote(st, st_sib, sib_send, sib_recv, sib)
    ycopies = [remote(st_y.at[0], st_y.at[d], sy_send.at[d], sy_recv.at[d], ypeers[d - 1]) for d in range(1, NY)]
    xcopies = [remote(st_x.at[0], st_x.at[d], sx_send.at[d], sx_recv.at[d], xpeers[d - 1]) for d in range(1, NX)]
    zcopies = [remote(st_z.at[z], st_z.at[z], sz_send.at[k], sz_recv.at[k], dev) for k, dev in enumerate(zpeers)]
    sib_copy.start()
    sib_copy.wait_recv()
    st_y[0] = merge([st[...], st_sib[...]])
    for g in ycopies:
        g.start()

    def ag_next(i, s):
        for d in (0, 1):
            ag_wait(d, i, s - 1)
            ag(d, i, s).start()

    def ag_two(i, _):
        ag_next(i, 2)

        @pl.when(i == 1)
        def _():
            for g in ycopies:
                g.wait_recv()
            st_x[0] = merge([st_y[d] for d in range(NY)])
            for g in xcopies:
                g.start()

        @pl.when(i == 3)
        def _():
            for g in xcopies:
                g.wait_recv()
            st_z[z, 0:16] = merge([st_x[d] for d in range(NX)])
            for g in zcopies:
                g.start()

        return 0

    lax.fori_loop(0, NX, ag_two, 0)

    def settle():
        for k in range(NZ - 1):
            o = zmod(z - 1 - k)
            remote(st_z.at[o], st_z.at[o], sz_send.at[k], sz_recv.at[k], sib).wait_recv()
        lab_hop(0, 4).wait_recv()
        hess_copy.wait()
        far_copy.wait()
        st_f[...] = merge([st_z[o, 0:16] for o in range(NZ)])
        for r in range(8):
            lab_t[r : r + 1, :] = lab_v[r]
        lab_t[8:16] = swap(lab_t[0:8])
        for r in range(8):
            a, b = chip_of(2 * r), chip_of(2 * r + 1)
            st_l[r : r + 1, :] = st_f[pl.ds(a, 1), :]
            st_l[8 + r : 9 + r, :] = st_f[pl.ds(b, 1), :]
            lab_l[r : r + 1, :] = jnp.where(
                left8[0:1], lab_t[pl.ds(a // 2 + 8 * lax.rem(a, 2), 1), :], lab_t[pl.ds(b // 2 + 8 * (1 - lax.rem(b, 2)), 1), :]
            )
        a, b = st_l[0:8], st_l[8:16]
        stat[0:8] = jnp.where(left8, a, swap(b))
        stat[8:16] = 1.0 / jnp.where(left8, swap(a), b)

    def prep(o, i):
        base = v * (NZ * OWN) + o * OWN
        for h in range(2):
            r = 2 * i + h
            top, inv = stat[pl.ds(r, 1), :], stat[pl.ds(8 + r, 1), :]
            scale = st_z[o, pl.ds(16 + r, 1), :]
            lab = lab_l[pl.ds(r, 1), :]
            for q in range(4):
                sub = slice(64 * q, 64 * (q + 1))
                l = lg[o, i, sub, 128 * h : 128 * (h + 1)].astype(F32) * scale
                p = jnp.exp(l - top) * inv
                ids = base + 64 * q + lax.broadcasted_iota(jnp.int32, (64, 128), 0)
                lanes = pl.ds(pl.multiple_of(256 * i + 128 * h, 128), 128)
                res[sub, lanes] = (p - (ids == lab).astype(F32)).astype(BF16)

    def tile(o, n):
        cols = pl.ds(pl.multiple_of(n * 256, 256), 256)
        rws = pl.ds(pl.multiple_of(o * OWN, OWN), OWN)
        sums = jnp.dot(res[...], h_v[:, cols], preferred_element_type=F32)
        out_ref[rws, cols] = step_of(sums, hess_v[rws, cols])

    def last(k, _):
        @pl.when(k < NX)
        def _():
            ag_next(k, 3)

        @pl.when(k == 0)
        def _():
            settle()

        @pl.when((k >= NX) & (k < 2 * NX))
        def _():
            ag_next(k - NX, 4)

        u = jnp.where(k < 6, k - 1, k - 3)
        o = zmod(z + ((u + 1) // 2) * (1 - 2 * lax.rem(u + 2, 2)))

        @pl.when(((k >= 1) & (k < 6)) | (k >= 8))
        def _():
            def preps(i, _):
                @pl.when(k == 10)
                def _():
                    for d in (0, 1):
                        ag_wait(d, i, 4)

                prep(o, i)
                return 0

            lax.fori_loop(0, NX, preps, 0)

            def tiles(n, _):
                tile(o, n)
                return 0

            @pl.when(k < 10)
            def _():
                lax.fori_loop(0, WIDTH // 256, tiles, 0)

        return 0

    lax.fori_loop(0, 11, last, 0)

    for c in range(5, 16):
        remote(slot(c, core), slot(c, core), g_send.at[c], g_recv.at[c], sib).wait_send()
    for k in range(16):
        share(k).wait_send()
    for g in [sib_copy] + ycopies + xcopies + zcopies:
        g.wait_send()
    for step in (1, 2, 3, 4):
        for d in (0, 1):
            if step < 4 or d == 0:
                lab_hop(d, step).wait_send()

    def finish(xs, _):
        for d in (0, 1):
            for s in (1, 2, 3, 4):
                rs_data(d, xs, s).wait_send()
                rs_bound(d, xs, s).wait_send()
                ag(d, xs, s).wait_send()
        return 0

    lax.fori_loop(0, NX, finish, 0)


def finish_kernel(done, res, h_v, hess_l, out_ref, ob, sem):
    z = lax.axis_index("dp")
    o = lax.rem(z + 4, NZ)

    def rows_at(k):
        return pl.ds(pl.multiple_of(k * OWN, OWN), OWN)

    copies = []
    for k in range(1, NZ):
        rws = rows_at(lax.rem(o + k, NZ))
        copies.append(pltpu.make_async_copy(done.at[rws], out_ref.at[rws], sem.at[k]))
        copies[-1].start()
    for n in range(WIDTH // 256):
        cols = slice(256 * n, 256 * (n + 1))
        sums = jnp.dot(res[...], h_v[:, cols], preferred_element_type=F32)
        ob[:, cols] = step_of(sums, hess_l[:, cols])
        copies.append(pltpu.make_async_copy(ob.at[:, cols], out_ref.at[rows_at(o), cols], sem.at[NZ + n]))
        copies[-1].start()
    for c in copies:
        c.wait()


def local(hidden, labels, head_weight, hess_old):
    dma = pltpu.SemaphoreType.DMA
    vmem = pl.BlockSpec(memory_space=pltpu.VMEM)
    parts = pl.pallas_call(
        kernel,
        out_shape=(
            pltpu.VMEM(hess_old.shape, BF16),
            pltpu.VMEM((OWN, TOK), BF16),
            pltpu.VMEM((TOK, WIDTH), BF16),
            pltpu.VMEM((OWN, WIDTH), BF16),
        ),
        in_specs=[pl.BlockSpec(memory_space=pltpu.HBM)] * 4,
        out_specs=(vmem,) * 4,
        scratch_shapes=[
            pltpu.VMEM((NZ * OWN, WIDTH), BF16),
            pltpu.VMEM((NZ * OWN, WIDTH), BF16),
            pltpu.VMEM((NZ, 1, 128), jnp.int32),
            pltpu.VMEM((16, 128), jnp.int32),
            pltpu.VMEM((8, 128), jnp.int32),
            pltpu.VMEM((NX, NZ, OWN, SB), F32),
            pltpu.VMEM((NX, NZ, 2, SB), F32),
            pltpu.VMEM((2, NX, 4, OWN, SB), I16),
            pltpu.VMEM((2, NX, HALF, SB), I16),
            pltpu.VMEM((2, NX, 5, 2, SB), F32),
            pltpu.VMEM((NZ, NX, OWN, SB), I16),
            pltpu.VMEM((16, 128), F32),
            pltpu.VMEM((16, 128), F32),
            pltpu.VMEM((16, 128), F32),
            pltpu.VMEM((16, 128), F32),
            pltpu.VMEM((NY, 16, 128), F32),
            pltpu.VMEM((NX, 16, 128), F32),
            pltpu.VMEM((NZ, 24, 128), F32),
            pltpu.VMEM((16, 128), F32),
            dma((5,)),
            dma((16,)), dma((16,)), dma((16,)), dma((16,)),
            dma((2, 4)), dma((2, 4)),
            dma((2, NX, 4)), dma((2, NX, 4)),
            dma((2, NX, 4)), dma((2, NX, 4)),
            dma((2, NX, 4)), dma((2, NX, 4)),
            dma((NY,)), dma((NY,)),
            dma((NX,)), dma((NX,)),
            dma, dma,
            dma((7,)), dma((7,)),
        ],
        compiler_params=pltpu.CompilerParams(
            collective_id=0, has_side_effects=True, vmem_limit_bytes=56 * 2**20
        ),
        cost_estimate=pl.CostEstimate(
            flops=8 * TOK * NZ * OWN * WIDTH, bytes_accessed=13 * 2**20, transcendentals=TOK * NZ * OWN
        ),
    )(hidden, labels.reshape(1, 128), head_weight, hess_old)
    parts = [pltpu.with_memory_space_constraint(p, pltpu.VMEM) for p in parts]
    return pl.pallas_call(
        finish_kernel,
        out_shape=jax.ShapeDtypeStruct(hess_old.shape, BF16),
        in_specs=[vmem] * 4,
        out_specs=pl.BlockSpec(memory_space=pl.ANY),
        scratch_shapes=[pltpu.VMEM((OWN, WIDTH), BF16), dma((NZ + WIDTH // 256,))],
        compiler_params=pltpu.CompilerParams(vmem_limit_bytes=16 * 2**20),
        cost_estimate=pl.CostEstimate(flops=2 * TOK * OWN * WIDTH, bytes_accessed=5 * 2**20, transcendentals=0),
    )(*parts)


def solution(mesh):
    in_specs = (P("vocab", "dp"), P("dp"), P("vocab", "dp"), P("vocab", "dp"))
    out_specs = P("vocab", "dp")
    return jax.shard_map(local, mesh=mesh, in_specs=in_specs, out_specs=out_specs, check_vma=False)
```

```python
import functools

import jax
import jax.numpy as jnp
from jax import lax
from jax.experimental import pallas as pl
from jax.experimental.pallas import tpu as pltpu
from jax.sharding import PartitionSpec as P

MESH = pl.DeviceIdType.MESH
F32, BF16, I16 = jnp.float32, jnp.bfloat16, jnp.int16
NZ, NX, NY = 8, 4, 4
OWN = 256
HALF = 128
SB = 256
TOK = 1024
WIDTH = 1024
BLK = 32
TOP = 32760.0
TINY = 1e-30
SLOTS = (
    (0, 0), (0, 1), (0, 3), (1, 0),
    (3, 0), (1, 1), (3, 3), (1, 3),
    (3, 1), (2, 0), (0, 2), (2, 1),
    (2, 3), (1, 2), (3, 2), (2, 2),
)
HOPS = {
    0: (
        (1, (0, 1)), (2, (0, 3)), (3, (1, 0)), (4, (3, 0)),
        (5, (1, 1)), (6, (3, 3)), (7, (1, 3)), (8, (3, 1)),
    ),
    1: ((10, (0, 1)),),
    3: ((9, (1, 0)),),
    5: ((11, (1, 0)),),
    6: ((12, (3, 0)),),
    7: ((13, (0, 3)),),
    8: ((14, (0, 1)),),
    14: ((15, (3, 0)),),
}
ARRIVE = ((1, 2, 3, 4), (5, 6, 7, 8), (9, 10, 11, 12, 13, 14), (15,))
ORDER = ((1, 0), (1, 1), (2, 0), (1, 2), (2, 1), (1, 3), (2, 2), (3, 0), (2, 3), (3, 1), (3, 2), (3, 3))


def pick(k, values):
    out = values[0]
    for j in range(1, len(values)):
        out = jnp.where(k == j, values[j], out)
    return out


def step_of(sums, old):
    scaled = 9000.0 * old.astype(F32) + 1000.0 * sums * sums
    return jnp.clip(sums / scaled, -1.0, 1.0).astype(BF16)


def kernel(
    hid_ref, lab_ref, w_ref, hess_ref, out_ref, res, h_v, hess_l,
    w_v, hess_v, lab_v, lab_t, lab_l, part, mb, rb, rf, bb, lg, st_l, st, st_f, st_sib, st_y, st_q, st_x, st_z, bd, stat,
    loc_sem, g_send, g_recv, f_send, f_recv, lab_send, lab_recv, rs_send, rs_recv, bs_send, bs_recv,
    ag_send, ag_recv, sy_send, sy_recv, sx_send, sx_recv, sf_send, sf_recv, bd_send, bd_recv, sib_send, sib_recv, sz_send, sz_recv,
):
    z = lax.axis_index("dp")
    v = lax.axis_index("vocab")
    core = lax.rem(v, 2)
    chip = v // 2
    x, y = chip // NY, lax.rem(chip, NY)
    sib = (z, v + 1 - 2 * core)

    def zmod(a):
        return lax.rem(a + 2 * NZ, NZ)

    def at(dx, dy):
        return (z, (lax.rem(x + dx, NX) * NY + lax.rem(y + dy, NY)) * 2 + core)

    def chip_of(k):
        dx, dy = SLOTS[k]
        return lax.rem(x + NX - dx, NX) * NY + lax.rem(y + NY - dy, NY)

    def remote(src, dst, ssem, rsem, dev):
        return pltpu.make_async_remote_copy(
            src_ref=src, dst_ref=dst, send_sem=ssem, recv_sem=rsem, device_id=dev, device_id_type=MESH
        )

    w_copy = pltpu.make_async_copy(w_ref, w_v, loc_sem.at[0])
    hess_copy = pltpu.make_async_copy(hess_ref, hess_v, loc_sem.at[1])
    lab_copy = pltpu.make_async_copy(lab_ref, lab_v.at[z], loc_sem.at[2])

    def slot(k, co):
        return h_v.at[pl.ds(pl.multiple_of(k * 2 * BLK + co * BLK, BLK), BLK)]

    far = pl.ds(pl.multiple_of(zmod(z + 4) * OWN, OWN), OWN)
    far_copy = pltpu.make_async_copy(hess_ref.at[far], hess_l, loc_sem.at[4])
    own_copy = pltpu.make_async_copy(hid_ref, slot(0, core), loc_sem.at[3])
    lab_copy.start()
    own_copy.start()

    zring = ((zmod(z + 1), v), (zmod(z - 1), v))
    zpeers = [(zmod(z + k), v) for k in range(1, NZ)]
    ypeers = [at(0, d) for d in range(1, NY)]
    xpeers = [at(d, 0) for d in range(1, NX)]

    barrier = pltpu.get_barrier_semaphore()
    partners = list(zring) + [at(0, 1), at(0, 3), at(1, 0), at(3, 0), sib]
    partners += [at(dx, dy) for dx in (1, 3) for dy in (1, 3)]
    for dev in partners:
        pl.semaphore_signal(barrier, inc=1, device_id=dev, device_id_type=MESH)
    pl.semaphore_wait(barrier, len(partners))

    def hop(k, c, step):
        src = slot(k, core)
        return remote(src, slot(c, core), g_send.at[c], g_recv.at[c], at(*step))

    def share(k):
        src = hid_ref if k == 0 else slot(k, core)
        return remote(src, slot(k, core), f_send.at[k], f_recv.at[k], sib)

    own_copy.wait()
    for c, step in HOPS[0][:4]:
        hop(0, c, step).start()
    share(0).start()
    w_copy.start()
    def lab_hop(d, step):
        o = zmod(z + 1 - step) if d == 0 else zmod(z - 1 + step)
        return remote(lab_v.at[o], lab_v.at[o], lab_send.at[d, step - 1], lab_recv.at[d, step - 1], zring[d])

    lab_copy.wait()
    for d in (0, 1):
        lab_hop(d, 1).start()
    w_copy.wait()
    for c, step in HOPS[0][:4]:
        hop(0, c, step).wait_send()
    for c, step in HOPS[0][4:]:
        hop(0, c, step).start()

    def gather_group(i):
        for k in ARRIVE[i]:
            remote(slot(k, core), slot(k, core), g_send.at[k], g_recv.at[k], sib).wait_recv()
            for c, step in HOPS.get(k, ()):
                hop(k, c, step).start()
            share(k).start()
        for k in range(4 * i, 4 * i + 4):
            remote(slot(k, 1 - core), slot(k, 1 - core), f_send.at[k], f_recv.at[k], sib).wait_recv()

    def mm(xs, o):
        a = w_v[pl.ds(pl.multiple_of(o * OWN, OWN), OWN), :]
        b = h_v[pl.ds(pl.multiple_of(xs * SB, SB), SB), :]
        p = lax.dot_general(a, b, (((1,), (1,)), ((), ())), preferred_element_type=F32)
        part[xs, o] = p
        mb[xs, o, 0:1, :] = jnp.max(jnp.abs(p[:HALF]), axis=0, keepdims=True)
        mb[xs, o, 1:2, :] = jnp.max(jnp.abs(p[HALF:]), axis=0, keepdims=True)

    def rows_of(xs, o, half):
        return part[xs, o, half * HALF : (half + 1) * HALF, :]

    def to_int(q):
        return jnp.round(q).astype(I16)

    def first(d, xs, far_o, next_o):
        b = jnp.maximum(mb[xs, far_o, d : d + 1, :], mb[xs, next_o, 1 - d : 2 - d, :])
        scale = TOP / jnp.maximum(b, TINY)
        rb[d, xs, 0, :HALF, :] = to_int(rows_of(xs, far_o, d) * scale)
        rb[d, xs, 0, HALF:, :] = to_int(rows_of(xs, next_o, 1 - d) * scale)
        bb[d, xs, 0] = b

    def fold(d, xs, slot, far_o, next_o):
        b_in = bb[d, xs, slot]
        b = mb[xs, far_o, d : d + 1, :]
        if next_o is not None:
            b = jnp.maximum(b, mb[xs, next_o, 1 - d : 2 - d, :])
        b = b_in + b
        inv = 1.0 / jnp.maximum(b, TINY)
        old, new = b_in * inv, TOP * inv
        upper = rb[d, xs, slot, :HALF, :].astype(F32)
        rb[d, xs, slot, :HALF, :] = to_int(upper * old + rows_of(xs, far_o, d) * new)
        if next_o is None:
            bb[d, xs, 5] = b
            return
        lower = rb[d, xs, slot, HALF:, :].astype(F32)
        rb[d, xs, slot, HALF:, :] = to_int(lower * old + rows_of(xs, next_o, 1 - d) * new)
        bb[d, xs, slot] = b

    def rs_data(d, xs, s):
        if not isinstance(s, int) or s < 4:
            src, dst = rb.at[d, xs, s - 1], rb.at[d, xs, s]
        else:
            src, dst = rb.at[d, xs, 3, pl.ds(0, HALF)], rf.at[d, xs]
        return remote(src, dst, rs_send.at[d, xs, s - 1], rs_recv.at[d, xs, s - 1], zring[d])

    def rs_bound(d, xs, s):
        src = bb.at[d, xs, 5] if isinstance(s, int) and s == 4 else bb.at[d, xs, s - 1]
        return remote(src, bb.at[d, xs, s], bs_send.at[d, xs, s - 1], bs_recv.at[d, xs, s - 1], zring[d])

    def rs_start(d, xs, s):
        rs_bound(d, xs, s).start()
        rs_data(d, xs, s).start()

    def rs_wait(d, xs, s):
        rs_bound(d, xs, s).wait_recv()
        rs_data(d, xs, s).wait_recv()

    def event(k, _):
        s = pick(k, [e[0] for e in ORDER])
        i = pick(k, [e[1] for e in ORDER])

        for g in range(4):

            @pl.when((s == 1) & (i == g))
            def _(g=g):
                gather_group(g)

        @pl.when(s == 1)
        def _():
            def owners(j, _):
                mm(i, zmod(z + 3 + j))
                return 0

            lax.fori_loop(0, 2, owners, 0)
            first(0, i, zmod(z + 4), zmod(z + 3))
            rs_start(0, i, 1)
            lax.fori_loop(2, 3, owners, 0)
            first(1, i, zmod(z - 4), zmod(z - 3))
            rs_start(1, i, 1)

        @pl.when(s > 1)
        def _():
            def owners(j, _):
                mm(i, zmod(z + (4 - s) * (1 - 2 * j)))
                return 0

            lax.fori_loop(0, 2, owners, 0)
            rs_wait(0, i, s - 1)
            fold(0, i, s - 1, zmod(z + 5 - s), zmod(z + 4 - s))
            rs_start(0, i, s)
            rs_wait(1, i, s - 1)
            fold(1, i, s - 1, zmod(z - 5 + s), zmod(z - 4 + s))
            rs_start(1, i, s)

        for step in (1, 2, 3):

            @pl.when(k == 3 * step)
            def _(step=step):
                for d in (0, 1):
                    lab_hop(d, step).wait_recv()
                    if step < 3 or d == 0:
                        lab_hop(d, step + 1).start()

        return 0

    lax.fori_loop(0, len(ORDER), event, 0)

    hess_copy.start()
    far_copy.start()

    def step4(i, _):
        xs = i
        rs_wait(0, xs, 3)
        fold(0, xs, 3, zmod(z + 1), None)
        rs_start(0, xs, 4)
        rs_wait(1, xs, 3)
        fold(1, xs, 3, zmod(z - 1), None)
        rs_start(1, xs, 4)
        mm(xs, z)
        return 0

    lax.fori_loop(0, NX, step4, 0)

    def ag(d, xs, s):
        o = zmod(z + 1 - s) if d == 0 else zmod(z - 1 + s)
        ref = lg.at[o, xs]
        if s == 4:
            ref = lg.at[o, xs, pl.ds(d * HALF, HALF)]
        return remote(ref, ref, ag_send.at[d, xs, s - 1], ag_recv.at[d, xs, s - 1], zring[d])

    def ag_wait(d, xs, s):
        o = zmod(z - s) if d == 0 else zmod(z + s)
        ref = lg.at[o, xs]
        if s == 4:
            ref = lg.at[o, xs, pl.ds(d * HALF, HALF)]
        remote(ref, ref, ag_send.at[d, xs, s - 1], ag_recv.at[d, xs, s - 1], zring[d]).wait_recv()

    def total(i, _):
        xs = i
        rs_wait(0, xs, 4)
        rs_wait(1, xs, 4)
        b0, b1 = bb[0, xs, 4], bb[1, xs, 3]
        c0, c1 = bb[1, xs, 4], bb[0, xs, 3]
        k = 1.0 / TOP
        upper = rows_of(xs, z, 0) + rf[0, xs].astype(F32) * (b0 * k) + rb[1, xs, 3, HALF:, :].astype(F32) * (b1 * k)
        lower = rows_of(xs, z, 1) + rf[1, xs].astype(F32) * (c0 * k) + rb[0, xs, 3, HALF:, :].astype(F32) * (c1 * k)
        b = jnp.maximum(mb[xs, z, 0:1, :] + b0 + b1, mb[xs, z, 1:2, :] + c0 + c1)
        b = jnp.maximum(b, TINY)
        scale = TOP / b
        lg[z, xs, :HALF, :] = to_int(upper * scale)
        lg[z, xs, HALF:, :] = to_int(lower * scale)
        ag(0, xs, 1).start()
        ag(1, xs, 1).start()
        m = jnp.maximum(jnp.max(upper, axis=0, keepdims=True), jnp.max(lower, axis=0, keepdims=True))
        e = jnp.sum(jnp.exp(upper - m), axis=0, keepdims=True) + jnp.sum(jnp.exp(lower - m), axis=0, keepdims=True)
        for j in range(2):
            lanes = slice(128 * j, 128 * (j + 1))
            st_l[pl.ds(2 * xs + j, 1), :] = m[:, lanes]
            st_l[pl.ds(8 + 2 * xs + j, 1), :] = e[:, lanes]
            bd[z, pl.ds(2 * xs + j, 1), :] = b[:, lanes] * k
        return 0

    lax.fori_loop(0, NX, total, 0)

    left8 = lax.broadcasted_iota(jnp.int32, (8, 128), 1) < 64

    def swap(a):
        return pltpu.roll(a, 64, 1)

    def merge(parts):
        m = parts[0]
        for a in parts[1:]:
            m = jnp.maximum(m, a)
        e = jnp.zeros_like(m)
        for a in parts:
            e = e + a * swap(jnp.exp(a - m))
        return jnp.where(lax.broadcasted_iota(jnp.int32, m.shape, 1) < 64, m, e)

    m, e = st_l[0:8], st_l[8:16]
    even, odd = jnp.where(left8, m, swap(e)), jnp.where(left8, swap(m), e)
    for r in range(8):
        st[pl.ds(chip_of(2 * r), 1), :] = even[r : r + 1]
        st[pl.ds(chip_of(2 * r + 1), 1), :] = odd[r : r + 1]

    sib_copy = remote(st, st_sib, sib_send, sib_recv, sib)
    ycopies = [remote(st_y.at[0], st_y.at[d], sy_send.at[d], sy_recv.at[d], ypeers[d - 1]) for d in range(1, NY)]
    xcopies = [
        remote(st_q.at[lax.rem(x + d, NX)], st_x.at[d], sx_send.at[d], sx_recv.at[d], xpeers[d - 1]) for d in range(1, NX)
    ]
    zcopies = [remote(st_z.at[z], st_z.at[z], sz_send.at[k], sz_recv.at[k], dev) for k, dev in enumerate(zpeers)]
    bcopies = [remote(bd.at[z], bd.at[z], bd_send.at[k], bd_recv.at[k], dev) for k, dev in enumerate(zpeers)]
    fcopies = [remote(st_f.at[x], st_f.at[x], sf_send.at[d], sf_recv.at[d], xpeers[d - 1]) for d in range(1, NX)]
    sib_copy.start()
    sib_copy.wait_recv()
    st_y[0] = merge([st[...], st_sib[...]])
    for g in ycopies + bcopies:
        g.start()

    def ag_next(i, s):
        for d in (0, 1):
            ag_wait(d, i, s - 1)
            ag(d, i, s).start()

    def ag_two(i, _):
        ag_next(i, 2)

        @pl.when(i == 1)
        def _():
            for g in ycopies:
                g.wait_recv()
            m = merge([st_y[d] for d in range(NY)])
            for c in range(NX):
                st_q[c] = m[NY * c : NY * (c + 1)]
            st_x[0] = st_q[x]
            for g in xcopies:
                g.start()

        @pl.when(i == 2)
        def _():
            for g in xcopies:
                g.wait_recv()
            st_z[z] = merge([st_x[d] for d in range(NX)])
            for g in zcopies:
                g.start()

        return 0

    lax.fori_loop(0, NX, ag_two, 0)

    def cross():
        for k in range(NZ - 1):
            o = zmod(z - 1 - k)
            remote(st_z.at[o], st_z.at[o], sz_send.at[k], sz_recv.at[k], sib).wait_recv()
        st_f[x] = merge([st_z[o] for o in range(NZ)])
        for g in fcopies:
            g.start()

    def settle():
        for d in range(1, NX):
            c = lax.rem(x + NX - d, NX)
            remote(st_f.at[c], st_f.at[c], sf_send.at[d], sf_recv.at[d], sib).wait_recv()
        for k in range(NZ - 1):
            o = zmod(z - 1 - k)
            remote(bd.at[o], bd.at[o], bd_send.at[k], bd_recv.at[k], sib).wait_recv()
        lab_hop(0, 4).wait_recv()
        hess_copy.wait()
        far_copy.wait()
        for r in range(8):
            lab_t[r : r + 1, :] = lab_v[r]
        lab_t[8:16] = swap(lab_t[0:8])
        for r in range(8):
            a, b = chip_of(2 * r), chip_of(2 * r + 1)
            st_l[r : r + 1, :] = st_f[a // NY, pl.ds(lax.rem(a, NY), 1), :]
            st_l[8 + r : 9 + r, :] = st_f[b // NY, pl.ds(lax.rem(b, NY), 1), :]
            lab_l[r : r + 1, :] = jnp.where(
                left8[0:1], lab_t[pl.ds(a // 2 + 8 * lax.rem(a, 2), 1), :], lab_t[pl.ds(b // 2 + 8 * (1 - lax.rem(b, 2)), 1), :]
            )
        a, b = st_l[0:8], st_l[8:16]
        stat[0:8] = jnp.where(left8, a, swap(b))
        stat[8:16] = 1.0 / jnp.where(left8, swap(a), b)

    def prep(o, i):
        base = v * (NZ * OWN) + o * OWN
        for h in range(2):
            r = 2 * i + h
            top, inv = stat[pl.ds(r, 1), :], stat[pl.ds(8 + r, 1), :]
            scale = bd[o, pl.ds(r, 1), :]
            lab = lab_l[pl.ds(r, 1), :]
            for q in range(4):
                sub = slice(64 * q, 64 * (q + 1))
                l = lg[o, i, sub, 128 * h : 128 * (h + 1)].astype(F32) * scale
                p = jnp.exp(l - top) * inv
                ids = base + 64 * q + lax.broadcasted_iota(jnp.int32, (64, 128), 0)
                lanes = pl.ds(pl.multiple_of(256 * i + 128 * h, 128), 128)
                res[sub, lanes] = (p - (ids == lab).astype(F32)).astype(BF16)

    def tile(o, n):
        cols = pl.ds(pl.multiple_of(n * 256, 256), 256)
        rws = pl.ds(pl.multiple_of(o * OWN, OWN), OWN)
        sums = jnp.dot(res[...], h_v[:, cols], preferred_element_type=F32)
        out_ref[rws, cols] = step_of(sums, hess_v[rws, cols])

    def last(k, _):
        @pl.when(k < NX)
        def _():
            ag_next(k, 3)

        @pl.when(k == 0)
        def _():
            cross()

        @pl.when(k == 1)
        def _():
            settle()

        @pl.when((k >= NX) & (k < 2 * NX))
        def _():
            ag_next(k - NX, 4)

        u = jnp.where(k < 6, k - 1, k - 3)
        o = zmod(z + ((u + 1) // 2) * (1 - 2 * lax.rem(u + 2, 2)))

        @pl.when(((k >= 1) & (k < 6)) | (k >= 8))
        def _():
            def preps(i, _):
                @pl.when(k == 10)
                def _():
                    for d in (0, 1):
                        ag_wait(d, i, 4)

                prep(o, i)
                return 0

            lax.fori_loop(0, NX, preps, 0)

            def tiles(n, _):
                tile(o, n)
                return 0

            @pl.when(k < 10)
            def _():
                lax.fori_loop(0, WIDTH // 256, tiles, 0)

        return 0

    lax.fori_loop(0, 11, last, 0)

    for c in range(5, 16):
        remote(slot(c, core), slot(c, core), g_send.at[c], g_recv.at[c], sib).wait_send()
    for k in range(16):
        share(k).wait_send()
    for g in [sib_copy] + ycopies + xcopies + zcopies + bcopies + fcopies:
        g.wait_send()
    for step in (1, 2, 3, 4):
        for d in (0, 1):
            if step < 4 or d == 0:
                lab_hop(d, step).wait_send()

    def finish(xs, _):
        for d in (0, 1):
            for s in (1, 2, 3, 4):
                rs_data(d, xs, s).wait_send()
                rs_bound(d, xs, s).wait_send()
                ag(d, xs, s).wait_send()
        return 0

    lax.fori_loop(0, NX, finish, 0)


def finish_kernel(done, res, h_v, hess_l, out_ref, ob, sem):
    z = lax.axis_index("dp")
    o = lax.rem(z + 4, NZ)

    def rows_at(k):
        return pl.ds(pl.multiple_of(k * OWN, OWN), OWN)

    copies = []
    for k in range(1, NZ):
        rws = rows_at(lax.rem(o + k, NZ))
        copies.append(pltpu.make_async_copy(done.at[rws], out_ref.at[rws], sem.at[k]))
        copies[-1].start()
    for n in range(WIDTH // 256):
        cols = slice(256 * n, 256 * (n + 1))
        sums = jnp.dot(res[...], h_v[:, cols], preferred_element_type=F32)
        ob[:, cols] = step_of(sums, hess_l[:, cols])
        copies.append(pltpu.make_async_copy(ob.at[:, cols], out_ref.at[rows_at(o), cols], sem.at[NZ + n]))
        copies[-1].start()
    for c in copies:
        c.wait()


def local(hidden, labels, head_weight, hess_old):
    dma = pltpu.SemaphoreType.DMA
    vmem = pl.BlockSpec(memory_space=pltpu.VMEM)
    parts = pl.pallas_call(
        kernel,
        out_shape=(
            pltpu.VMEM(hess_old.shape, BF16),
            pltpu.VMEM((OWN, TOK), BF16),
            pltpu.VMEM((TOK, WIDTH), BF16),
            pltpu.VMEM((OWN, WIDTH), BF16),
        ),
        in_specs=[pl.BlockSpec(memory_space=pltpu.HBM)] * 4,
        out_specs=(vmem,) * 4,
        scratch_shapes=[
            pltpu.VMEM((NZ * OWN, WIDTH), BF16),
            pltpu.VMEM((NZ * OWN, WIDTH), BF16),
            pltpu.VMEM((NZ, 1, 128), jnp.int32),
            pltpu.VMEM((16, 128), jnp.int32),
            pltpu.VMEM((8, 128), jnp.int32),
            pltpu.VMEM((NX, NZ, OWN, SB), F32),
            pltpu.VMEM((NX, NZ, 2, SB), F32),
            pltpu.VMEM((2, NX, 4, OWN, SB), I16),
            pltpu.VMEM((2, NX, HALF, SB), I16),
            pltpu.VMEM((2, NX, 6, 1, SB), F32),
            pltpu.VMEM((NZ, NX, OWN, SB), I16),
            pltpu.VMEM((16, 128), F32),
            pltpu.VMEM((16, 128), F32),
            pltpu.VMEM((NX, NY, 128), F32),
            pltpu.VMEM((16, 128), F32),
            pltpu.VMEM((NY, 16, 128), F32),
            pltpu.VMEM((NX, NY, 128), F32),
            pltpu.VMEM((NX, NY, 128), F32),
            pltpu.VMEM((NZ, NY, 128), F32),
            pltpu.VMEM((NZ, 8, 128), F32),
            pltpu.VMEM((16, 128), F32),
            dma((5,)),
            dma((16,)), dma((16,)), dma((16,)), dma((16,)),
            dma((2, 4)), dma((2, 4)),
            dma((2, NX, 4)), dma((2, NX, 4)),
            dma((2, NX, 4)), dma((2, NX, 4)),
            dma((2, NX, 4)), dma((2, NX, 4)),
            dma((NY,)), dma((NY,)),
            dma((NX,)), dma((NX,)),
            dma((NX,)), dma((NX,)),
            dma((7,)), dma((7,)),
            dma, dma,
            dma((7,)), dma((7,)),
        ],
        compiler_params=pltpu.CompilerParams(
            collective_id=0, has_side_effects=True, vmem_limit_bytes=56 * 2**20
        ),
        cost_estimate=pl.CostEstimate(
            flops=8 * TOK * NZ * OWN * WIDTH, bytes_accessed=13 * 2**20, transcendentals=TOK * NZ * OWN
        ),
    )(hidden, labels.reshape(1, 128), head_weight, hess_old)
    parts = [pltpu.with_memory_space_constraint(p, pltpu.VMEM) for p in parts]
    return pl.pallas_call(
        finish_kernel,
        out_shape=jax.ShapeDtypeStruct(hess_old.shape, BF16),
        in_specs=[vmem] * 4,
        out_specs=pl.BlockSpec(memory_space=pl.ANY),
        scratch_shapes=[pltpu.VMEM((OWN, WIDTH), BF16), dma((NZ + WIDTH // 256,))],
        compiler_params=pltpu.CompilerParams(vmem_limit_bytes=16 * 2**20),
        cost_estimate=pl.CostEstimate(flops=2 * TOK * OWN * WIDTH, bytes_accessed=5 * 2**20, transcendentals=0),
    )(*parts)


def solution(mesh):
    in_specs = (P("vocab", "dp"), P("dp"), P("vocab", "dp"), P("vocab", "dp"))
    out_specs = P("vocab", "dp")
    return jax.shard_map(local, mesh=mesh, in_specs=in_specs, out_specs=out_specs, check_vma=False)
```

```python
import functools

import jax
import jax.numpy as jnp
from jax import lax
from jax.experimental import pallas as pl
from jax.experimental.pallas import tpu as pltpu
from jax.sharding import PartitionSpec as P

MESH = pl.DeviceIdType.MESH
F32, BF16, I16 = jnp.float32, jnp.bfloat16, jnp.int16
NZ, NX, NY = 8, 4, 4
OWN = 256
HALF = 128
SB = 256
TOK = 1024
WIDTH = 1024
BLK = 32
TOP = 32760.0
TINY = 1e-30
SLOTS = (
    (0, 0), (0, 1), (0, 3), (1, 0),
    (3, 0), (1, 1), (3, 3), (1, 3),
    (3, 1), (2, 0), (0, 2), (2, 1),
    (2, 3), (1, 2), (3, 2), (2, 2),
)
HOPS = {
    0: (
        (1, (0, 1)), (2, (0, 3)), (3, (1, 0)), (4, (3, 0)),
        (5, (1, 1)), (6, (3, 3)), (7, (1, 3)), (8, (3, 1)),
    ),
    1: ((10, (0, 1)),),
    3: ((9, (1, 0)),),
    5: ((11, (1, 0)),),
    6: ((12, (3, 0)),),
    7: ((13, (0, 3)),),
    8: ((14, (0, 1)),),
    14: ((15, (3, 0)),),
}
ARRIVE = ((1, 2, 3, 4), (5, 6, 7, 8), (9, 10, 11, 12, 13, 14), (15,))
ORDER = ((1, 0), (1, 1), (2, 0), (1, 2), (2, 1), (1, 3), (2, 2), (3, 0), (2, 3), (3, 1), (3, 2), (3, 3))


def pick(k, values):
    out = values[0]
    for j in range(1, len(values)):
        out = jnp.where(k == j, values[j], out)
    return out


def step_of(sums, old):
    scaled = 9000.0 * old.astype(F32) + 1000.0 * sums * sums
    return jnp.clip(sums / scaled, -1.0, 1.0).astype(BF16)


def kernel(
    hid_ref, lab_ref, w_ref, hess_ref, out_ref, res, h_v, hess_l,
    w_v, hess_v, lab_v, lab_t, lab_l, part, rb, rf, bb, lg, st_l, st, st_f, st_sib, st_y, st_q, st_x, st_z, bd, stat,
    loc_sem, g_send, g_recv, f_send, f_recv, lab_send, lab_recv, rs_send, rs_recv, bs_send, bs_recv,
    ag_send, ag_recv, sy_send, sy_recv, sx_send, sx_recv, sf_send, sf_recv, bd_send, bd_recv, sib_send, sib_recv, sz_send, sz_recv,
):
    z = lax.axis_index("dp")
    v = lax.axis_index("vocab")
    core = lax.rem(v, 2)
    chip = v // 2
    x, y = chip // NY, lax.rem(chip, NY)
    sib = (z, v + 1 - 2 * core)

    def zmod(a):
        return lax.rem(a + 2 * NZ, NZ)

    def at(dx, dy):
        return (z, (lax.rem(x + dx, NX) * NY + lax.rem(y + dy, NY)) * 2 + core)

    def chip_of(k):
        dx, dy = SLOTS[k]
        return lax.rem(x + NX - dx, NX) * NY + lax.rem(y + NY - dy, NY)

    def remote(src, dst, ssem, rsem, dev):
        return pltpu.make_async_remote_copy(
            src_ref=src, dst_ref=dst, send_sem=ssem, recv_sem=rsem, device_id=dev, device_id_type=MESH
        )

    w_copy = pltpu.make_async_copy(w_ref, w_v, loc_sem.at[0])
    hess_copy = pltpu.make_async_copy(hess_ref, hess_v, loc_sem.at[1])
    lab_copy = pltpu.make_async_copy(lab_ref, lab_v.at[z], loc_sem.at[2])

    def slot(k, co):
        return h_v.at[pl.ds(pl.multiple_of(k * 2 * BLK + co * BLK, BLK), BLK)]

    far = pl.ds(pl.multiple_of(zmod(z + 4) * OWN, OWN), OWN)
    far_copy = pltpu.make_async_copy(hess_ref.at[far], hess_l, loc_sem.at[4])
    own_copy = pltpu.make_async_copy(hid_ref, slot(0, core), loc_sem.at[3])
    lab_copy.start()
    own_copy.start()

    zring = ((zmod(z + 1), v), (zmod(z - 1), v))
    zpeers = [(zmod(z + k), v) for k in range(1, NZ)]
    ypeers = [at(0, d) for d in range(1, NY)]
    xpeers = [at(d, 0) for d in range(1, NX)]

    barrier = pltpu.get_barrier_semaphore()
    partners = list(zring) + [at(0, 1), at(0, 3), at(1, 0), at(3, 0), sib]
    partners += [at(dx, dy) for dx in (1, 3) for dy in (1, 3)]
    for dev in partners:
        pl.semaphore_signal(barrier, inc=1, device_id=dev, device_id_type=MESH)
    pl.semaphore_wait(barrier, len(partners))

    def hop(k, c, step):
        src = slot(k, core)
        return remote(src, slot(c, core), g_send.at[c], g_recv.at[c], at(*step))

    def share(k):
        src = hid_ref if k == 0 else slot(k, core)
        return remote(src, slot(k, core), f_send.at[k], f_recv.at[k], sib)

    own_copy.wait()
    for c, step in HOPS[0][:4]:
        hop(0, c, step).start()
    share(0).start()
    w_copy.start()
    def lab_hop(d, step):
        o = zmod(z + 1 - step) if d == 0 else zmod(z - 1 + step)
        return remote(lab_v.at[o], lab_v.at[o], lab_send.at[d, step - 1], lab_recv.at[d, step - 1], zring[d])

    lab_copy.wait()
    for d in (0, 1):
        lab_hop(d, 1).start()
    w_copy.wait()
    for c, step in HOPS[0][:4]:
        hop(0, c, step).wait_send()
    for c, step in HOPS[0][4:]:
        hop(0, c, step).start()

    def gather_group(i):
        for k in ARRIVE[i]:
            remote(slot(k, core), slot(k, core), g_send.at[k], g_recv.at[k], sib).wait_recv()
            for c, step in HOPS.get(k, ()):
                hop(k, c, step).start()
            share(k).start()
        for k in range(4 * i, 4 * i + 4):
            remote(slot(k, 1 - core), slot(k, 1 - core), f_send.at[k], f_recv.at[k], sib).wait_recv()

    def mm(xs, o):
        a = w_v[pl.ds(pl.multiple_of(o * OWN, OWN), OWN), :]
        b = h_v[pl.ds(pl.multiple_of(xs * SB, SB), SB), :]
        p = lax.dot_general(a, b, (((1,), (1,)), ((), ())), preferred_element_type=F32)
        part[xs, o] = p

    def rows_of(xs, o, half):
        return part[xs, o, half * HALF : (half + 1) * HALF, :]

    def largest(a):
        return jnp.maximum(jnp.max(jnp.abs(a), axis=0, keepdims=True), TINY)

    def to_int(q):
        return jnp.round(q).astype(I16)

    def first(d, xs, far_o, next_o):
        upper, lower = rows_of(xs, far_o, d), rows_of(xs, next_o, 1 - d)
        b = jnp.maximum(largest(upper), largest(lower))
        rb[d, xs, 0, :HALF, :] = to_int(upper * (TOP / b))
        rb[d, xs, 0, HALF:, :] = to_int(lower * (TOP / b))
        bb[d, xs, 0] = b * (1.0 / TOP)

    def fold(d, xs, slot, far_o, next_o):
        b_in = bb[d, xs, slot]
        upper = rb[d, xs, slot, :HALF, :].astype(F32) * b_in + rows_of(xs, far_o, d)
        b = largest(upper)
        if next_o is None:
            rb[d, xs, slot, :HALF, :] = to_int(upper * (TOP / b))
            bb[d, xs, 5] = b * (1.0 / TOP)
            return
        lower = rb[d, xs, slot, HALF:, :].astype(F32) * b_in + rows_of(xs, next_o, 1 - d)
        b = jnp.maximum(b, largest(lower))
        rb[d, xs, slot, :HALF, :] = to_int(upper * (TOP / b))
        rb[d, xs, slot, HALF:, :] = to_int(lower * (TOP / b))
        bb[d, xs, slot] = b * (1.0 / TOP)

    def rs_data(d, xs, s):
        if not isinstance(s, int) or s < 4:
            src, dst = rb.at[d, xs, s - 1], rb.at[d, xs, s]
        else:
            src, dst = rb.at[d, xs, 3, pl.ds(0, HALF)], rf.at[d, xs]
        return remote(src, dst, rs_send.at[d, xs, s - 1], rs_recv.at[d, xs, s - 1], zring[d])

    def rs_bound(d, xs, s):
        src = bb.at[d, xs, 5] if isinstance(s, int) and s == 4 else bb.at[d, xs, s - 1]
        return remote(src, bb.at[d, xs, s], bs_send.at[d, xs, s - 1], bs_recv.at[d, xs, s - 1], zring[d])

    def rs_start(d, xs, s):
        rs_bound(d, xs, s).start()
        rs_data(d, xs, s).start()

    def rs_wait(d, xs, s):
        rs_bound(d, xs, s).wait_recv()
        rs_data(d, xs, s).wait_recv()

    def event(k, _):
        s = pick(k, [e[0] for e in ORDER])
        i = pick(k, [e[1] for e in ORDER])

        for g in range(4):

            @pl.when((s == 1) & (i == g))
            def _(g=g):
                gather_group(g)

        @pl.when(s == 1)
        def _():
            def owners(j, _):
                mm(i, zmod(z + 3 + j))
                return 0

            lax.fori_loop(0, 2, owners, 0)
            first(0, i, zmod(z + 4), zmod(z + 3))
            rs_start(0, i, 1)
            lax.fori_loop(2, 3, owners, 0)
            first(1, i, zmod(z - 4), zmod(z - 3))
            rs_start(1, i, 1)

        @pl.when(s > 1)
        def _():
            def owners(j, _):
                mm(i, zmod(z + (4 - s) * (1 - 2 * j)))
                return 0

            lax.fori_loop(0, 2, owners, 0)
            rs_wait(0, i, s - 1)
            fold(0, i, s - 1, zmod(z + 5 - s), zmod(z + 4 - s))
            rs_start(0, i, s)
            rs_wait(1, i, s - 1)
            fold(1, i, s - 1, zmod(z - 5 + s), zmod(z - 4 + s))
            rs_start(1, i, s)

        for step in (1, 2, 3):

            @pl.when(k == 3 * step)
            def _(step=step):
                for d in (0, 1):
                    lab_hop(d, step).wait_recv()
                    if step < 3 or d == 0:
                        lab_hop(d, step + 1).start()

        return 0

    lax.fori_loop(0, len(ORDER), event, 0)

    hess_copy.start()
    far_copy.start()

    def step4(i, _):
        xs = i
        rs_wait(0, xs, 3)
        fold(0, xs, 3, zmod(z + 1), None)
        rs_start(0, xs, 4)
        rs_wait(1, xs, 3)
        fold(1, xs, 3, zmod(z - 1), None)
        rs_start(1, xs, 4)
        mm(xs, z)
        return 0

    lax.fori_loop(0, NX, step4, 0)

    def ag(d, xs, s):
        o = zmod(z + 1 - s) if d == 0 else zmod(z - 1 + s)
        ref = lg.at[o, xs]
        if s == 4:
            ref = lg.at[o, xs, pl.ds(d * HALF, HALF)]
        return remote(ref, ref, ag_send.at[d, xs, s - 1], ag_recv.at[d, xs, s - 1], zring[d])

    def ag_wait(d, xs, s):
        o = zmod(z - s) if d == 0 else zmod(z + s)
        ref = lg.at[o, xs]
        if s == 4:
            ref = lg.at[o, xs, pl.ds(d * HALF, HALF)]
        remote(ref, ref, ag_send.at[d, xs, s - 1], ag_recv.at[d, xs, s - 1], zring[d]).wait_recv()

    def total(i, _):
        xs = i
        rs_wait(0, xs, 4)
        rs_wait(1, xs, 4)
        b0, b1 = bb[0, xs, 4], bb[1, xs, 3]
        c0, c1 = bb[1, xs, 4], bb[0, xs, 3]
        upper = rows_of(xs, z, 0) + rf[0, xs].astype(F32) * b0 + rb[1, xs, 3, HALF:, :].astype(F32) * b1
        lower = rows_of(xs, z, 1) + rf[1, xs].astype(F32) * c0 + rb[0, xs, 3, HALF:, :].astype(F32) * c1
        b = jnp.maximum(largest(upper), largest(lower))
        scale = TOP / b
        lg[z, xs, :HALF, :] = to_int(upper * scale)
        lg[z, xs, HALF:, :] = to_int(lower * scale)
        ag(0, xs, 1).start()
        ag(1, xs, 1).start()
        m = jnp.maximum(jnp.max(upper, axis=0, keepdims=True), jnp.max(lower, axis=0, keepdims=True))
        e = jnp.sum(jnp.exp(upper - m), axis=0, keepdims=True) + jnp.sum(jnp.exp(lower - m), axis=0, keepdims=True)
        for j in range(2):
            lanes = slice(128 * j, 128 * (j + 1))
            st_l[pl.ds(2 * xs + j, 1), :] = m[:, lanes]
            st_l[pl.ds(8 + 2 * xs + j, 1), :] = e[:, lanes]
            bd[z, pl.ds(2 * xs + j, 1), :] = b[:, lanes] * (1.0 / TOP)
        return 0

    lax.fori_loop(0, NX, total, 0)

    left8 = lax.broadcasted_iota(jnp.int32, (8, 128), 1) < 64

    def swap(a):
        return pltpu.roll(a, 64, 1)

    def merge(parts):
        m = parts[0]
        for a in parts[1:]:
            m = jnp.maximum(m, a)
        e = jnp.zeros_like(m)
        for a in parts:
            e = e + a * swap(jnp.exp(a - m))
        return jnp.where(lax.broadcasted_iota(jnp.int32, m.shape, 1) < 64, m, e)

    m, e = st_l[0:8], st_l[8:16]
    even, odd = jnp.where(left8, m, swap(e)), jnp.where(left8, swap(m), e)
    for r in range(8):
        st[pl.ds(chip_of(2 * r), 1), :] = even[r : r + 1]
        st[pl.ds(chip_of(2 * r + 1), 1), :] = odd[r : r + 1]

    sib_copy = remote(st, st_sib, sib_send, sib_recv, sib)
    ycopies = [remote(st_y.at[0], st_y.at[d], sy_send.at[d], sy_recv.at[d], ypeers[d - 1]) for d in range(1, NY)]
    xcopies = [
        remote(st_q.at[lax.rem(x + d, NX)], st_x.at[d], sx_send.at[d], sx_recv.at[d], xpeers[d - 1]) for d in range(1, NX)
    ]
    zcopies = [remote(st_z.at[z], st_z.at[z], sz_send.at[k], sz_recv.at[k], dev) for k, dev in enumerate(zpeers)]
    bcopies = [remote(bd.at[z], bd.at[z], bd_send.at[k], bd_recv.at[k], dev) for k, dev in enumerate(zpeers)]
    fcopies = [remote(st_f.at[x], st_f.at[x], sf_send.at[d], sf_recv.at[d], xpeers[d - 1]) for d in range(1, NX)]
    sib_copy.start()
    sib_copy.wait_recv()
    st_y[0] = merge([st[...], st_sib[...]])
    for g in ycopies + bcopies:
        g.start()

    def ag_next(i, s):
        for d in (0, 1):
            ag_wait(d, i, s - 1)
            ag(d, i, s).start()

    def ag_two(i, _):
        ag_next(i, 2)

        @pl.when(i == 1)
        def _():
            for g in ycopies:
                g.wait_recv()
            m = merge([st_y[d] for d in range(NY)])
            for c in range(NX):
                st_q[c] = m[NY * c : NY * (c + 1)]
            st_x[0] = st_q[x]
            for g in xcopies:
                g.start()

        @pl.when(i == 2)
        def _():
            for g in xcopies:
                g.wait_recv()
            st_z[z] = merge([st_x[d] for d in range(NX)])
            for g in zcopies:
                g.start()

        return 0

    lax.fori_loop(0, NX, ag_two, 0)

    def cross():
        for k in range(NZ - 1):
            o = zmod(z - 1 - k)
            remote(st_z.at[o], st_z.at[o], sz_send.at[k], sz_recv.at[k], sib).wait_recv()
        st_f[x] = merge([st_z[o] for o in range(NZ)])
        for g in fcopies:
            g.start()

    def settle():
        for d in range(1, NX):
            c = lax.rem(x + NX - d, NX)
            remote(st_f.at[c], st_f.at[c], sf_send.at[d], sf_recv.at[d], sib).wait_recv()
        for k in range(NZ - 1):
            o = zmod(z - 1 - k)
            remote(bd.at[o], bd.at[o], bd_send.at[k], bd_recv.at[k], sib).wait_recv()
        lab_hop(0, 4).wait_recv()
        hess_copy.wait()
        far_copy.wait()
        for r in range(8):
            lab_t[r : r + 1, :] = lab_v[r]
        lab_t[8:16] = swap(lab_t[0:8])
        for r in range(8):
            a, b = chip_of(2 * r), chip_of(2 * r + 1)
            st_l[r : r + 1, :] = st_f[a // NY, pl.ds(lax.rem(a, NY), 1), :]
            st_l[8 + r : 9 + r, :] = st_f[b // NY, pl.ds(lax.rem(b, NY), 1), :]
            lab_l[r : r + 1, :] = jnp.where(
                left8[0:1], lab_t[pl.ds(a // 2 + 8 * lax.rem(a, 2), 1), :], lab_t[pl.ds(b // 2 + 8 * (1 - lax.rem(b, 2)), 1), :]
            )
        a, b = st_l[0:8], st_l[8:16]
        stat[0:8] = jnp.where(left8, a, swap(b))
        stat[8:16] = 1.0 / jnp.where(left8, swap(a), b)

    def prep(o, i):
        base = v * (NZ * OWN) + o * OWN
        for h in range(2):
            r = 2 * i + h
            top, inv = stat[pl.ds(r, 1), :], stat[pl.ds(8 + r, 1), :]
            scale = bd[o, pl.ds(r, 1), :]
            lab = lab_l[pl.ds(r, 1), :]
            for q in range(4):
                sub = slice(64 * q, 64 * (q + 1))
                l = lg[o, i, sub, 128 * h : 128 * (h + 1)].astype(F32) * scale
                p = jnp.exp(l - top) * inv
                ids = base + 64 * q + lax.broadcasted_iota(jnp.int32, (64, 128), 0)
                lanes = pl.ds(pl.multiple_of(256 * i + 128 * h, 128), 128)
                res[sub, lanes] = (p - (ids == lab).astype(F32)).astype(BF16)

    def tile(o, n):
        cols = pl.ds(pl.multiple_of(n * 256, 256), 256)
        rws = pl.ds(pl.multiple_of(o * OWN, OWN), OWN)
        sums = jnp.dot(res[...], h_v[:, cols], preferred_element_type=F32)
        out_ref[rws, cols] = step_of(sums, hess_v[rws, cols])

    def last(k, _):
        @pl.when(k < NX)
        def _():
            ag_next(k, 3)

        @pl.when(k == 0)
        def _():
            cross()

        @pl.when(k == 1)
        def _():
            settle()

        @pl.when((k >= NX) & (k < 2 * NX))
        def _():
            ag_next(k - NX, 4)

        u = jnp.where(k < 6, k - 1, k - 3)
        o = zmod(z + ((u + 1) // 2) * (1 - 2 * lax.rem(u + 2, 2)))

        @pl.when(((k >= 1) & (k < 6)) | (k >= 8))
        def _():
            def preps(i, _):
                @pl.when(k == 10)
                def _():
                    for d in (0, 1):
                        ag_wait(d, i, 4)

                prep(o, i)
                return 0

            lax.fori_loop(0, NX, preps, 0)

            def tiles(n, _):
                tile(o, n)
                return 0

            @pl.when(k < 10)
            def _():
                lax.fori_loop(0, WIDTH // 256, tiles, 0)

        return 0

    lax.fori_loop(0, 11, last, 0)

    for c in range(5, 16):
        remote(slot(c, core), slot(c, core), g_send.at[c], g_recv.at[c], sib).wait_send()
    for k in range(16):
        share(k).wait_send()
    for g in [sib_copy] + ycopies + xcopies + zcopies + bcopies + fcopies:
        g.wait_send()
    for step in (1, 2, 3, 4):
        for d in (0, 1):
            if step < 4 or d == 0:
                lab_hop(d, step).wait_send()

    def finish(xs, _):
        for d in (0, 1):
            for s in (1, 2, 3, 4):
                rs_data(d, xs, s).wait_send()
                rs_bound(d, xs, s).wait_send()
                ag(d, xs, s).wait_send()
        return 0

    lax.fori_loop(0, NX, finish, 0)


def finish_kernel(done, res, h_v, hess_l, out_ref, ob, sem):
    z = lax.axis_index("dp")
    o = lax.rem(z + 4, NZ)

    def rows_at(k):
        return pl.ds(pl.multiple_of(k * OWN, OWN), OWN)

    copies = []
    for k in range(1, NZ):
        rws = rows_at(lax.rem(o + k, NZ))
        copies.append(pltpu.make_async_copy(done.at[rws], out_ref.at[rws], sem.at[k]))
        copies[-1].start()
    for n in range(WIDTH // 256):
        cols = slice(256 * n, 256 * (n + 1))
        sums = jnp.dot(res[...], h_v[:, cols], preferred_element_type=F32)
        ob[:, cols] = step_of(sums, hess_l[:, cols])
        copies.append(pltpu.make_async_copy(ob.at[:, cols], out_ref.at[rows_at(o), cols], sem.at[NZ + n]))
        copies[-1].start()
    for c in copies:
        c.wait()


def local(hidden, labels, head_weight, hess_old):
    dma = pltpu.SemaphoreType.DMA
    vmem = pl.BlockSpec(memory_space=pltpu.VMEM)
    parts = pl.pallas_call(
        kernel,
        out_shape=(
            pltpu.VMEM(hess_old.shape, BF16),
            pltpu.VMEM((OWN, TOK), BF16),
            pltpu.VMEM((TOK, WIDTH), BF16),
            pltpu.VMEM((OWN, WIDTH), BF16),
        ),
        in_specs=[pl.BlockSpec(memory_space=pltpu.HBM)] * 4,
        out_specs=(vmem,) * 4,
        scratch_shapes=[
            pltpu.VMEM((NZ * OWN, WIDTH), BF16),
            pltpu.VMEM((NZ * OWN, WIDTH), BF16),
            pltpu.VMEM((NZ, 1, 128), jnp.int32),
            pltpu.VMEM((16, 128), jnp.int32),
            pltpu.VMEM((8, 128), jnp.int32),
            pltpu.VMEM((NX, NZ, OWN, SB), F32),
            pltpu.VMEM((2, NX, 4, OWN, SB), I16),
            pltpu.VMEM((2, NX, HALF, SB), I16),
            pltpu.VMEM((2, NX, 6, 1, SB), F32),
            pltpu.VMEM((NZ, NX, OWN, SB), I16),
            pltpu.VMEM((16, 128), F32),
            pltpu.VMEM((16, 128), F32),
            pltpu.VMEM((NX, NY, 128), F32),
            pltpu.VMEM((16, 128), F32),
            pltpu.VMEM((NY, 16, 128), F32),
            pltpu.VMEM((NX, NY, 128), F32),
            pltpu.VMEM((NX, NY, 128), F32),
            pltpu.VMEM((NZ, NY, 128), F32),
            pltpu.VMEM((NZ, 8, 128), F32),
            pltpu.VMEM((16, 128), F32),
            dma((5,)),
            dma((16,)), dma((16,)), dma((16,)), dma((16,)),
            dma((2, 4)), dma((2, 4)),
            dma((2, NX, 4)), dma((2, NX, 4)),
            dma((2, NX, 4)), dma((2, NX, 4)),
            dma((2, NX, 4)), dma((2, NX, 4)),
            dma((NY,)), dma((NY,)),
            dma((NX,)), dma((NX,)),
            dma((NX,)), dma((NX,)),
            dma((7,)), dma((7,)),
            dma, dma,
            dma((7,)), dma((7,)),
        ],
        compiler_params=pltpu.CompilerParams(
            collective_id=0, has_side_effects=True, vmem_limit_bytes=56 * 2**20
        ),
        cost_estimate=pl.CostEstimate(
            flops=8 * TOK * NZ * OWN * WIDTH, bytes_accessed=13 * 2**20, transcendentals=TOK * NZ * OWN
        ),
    )(hidden, labels.reshape(1, 128), head_weight, hess_old)
    parts = [pltpu.with_memory_space_constraint(p, pltpu.VMEM) for p in parts]
    return pl.pallas_call(
        finish_kernel,
        out_shape=jax.ShapeDtypeStruct(hess_old.shape, BF16),
        in_specs=[vmem] * 4,
        out_specs=pl.BlockSpec(memory_space=pl.ANY),
        scratch_shapes=[pltpu.VMEM((OWN, WIDTH), BF16), dma((NZ + WIDTH // 256,))],
        compiler_params=pltpu.CompilerParams(vmem_limit_bytes=16 * 2**20),
        cost_estimate=pl.CostEstimate(flops=2 * TOK * OWN * WIDTH, bytes_accessed=5 * 2**20, transcendentals=0),
    )(*parts)


def solution(mesh):
    in_specs = (P("vocab", "dp"), P("dp"), P("vocab", "dp"), P("vocab", "dp"))
    out_specs = P("vocab", "dp")
    return jax.shard_map(local, mesh=mesh, in_specs=in_specs, out_specs=out_specs, check_vma=False)
```
